512 devices in a mesh: seq: 128 (over z, x, core), doc: 4 (over y).
Axes of the slice: x: 4, y: 4, z: 16, core: 2. Of those that a mesh axis runs over, the one named last changes fastest.
Arguments:
- block_input: bfloat16 [4, 16384, 2048], P('doc', 'seq'), may hold values from -6 to 6
- state_cotangent: bfloat16 [4, 16384, 2048], P('doc', 'seq'), may hold values from -24 to 24
- recur_weight: bfloat16 [2048, 256], P('seq'), may hold values from -0.375 to 0.375
- input_weight: bfloat16 [2048, 256], P('seq'), may hold values from -0.375 to 0.375
- gate_bias: float32 [2, 2048], replicated, may hold values from -4 to 4
- conv_taps: float32 [4, 2048], replicated, may hold values from -3 to 3
- conv_bias: float32 [2048], replicated, may hold values from -3 to 3
- decay_param: float32 [2048], replicated, may hold values from 2 to 20
Outputs:
- input_grad: bfloat16 [4, 16384, 2048], P('doc', 'seq')
- recur_weight_grad: float32 [2048, 256], P('seq')
- input_weight_grad: float32 [2048, 256], P('seq')
- channel_grads: float32 [8, 2048], replicated
The draws below stay inside these ranges and needn't reach their ends.
All inputs are finite; a program needn't handle non-finite values.
Results may differ from the reference program's by a relative error of at most 0.008.
Values may be sent and summed in bfloat16 or wider, within the bound.
No kernel may reach another device: no remote copies, remote signals or barrier semaphores. Data moves between devices by JAX's collectives and lax.ppermute only.
A program may use at most 128 MiB of HBM per device.

```python
import jax
import jax.numpy as jnp
from jax import lax

WIDTH = 2048
BW = 256
TAPS = 4
TOKENS = 16384
DOCS = 4
NB = 8


def draw_decay_param(key, part):
    key = jax.random.fold_in(key, 11)
    low = jnp.log(0.25 / TOKENS)
    high = jnp.log(0.05)
    level = jax.random.uniform(key, (WIDTH,), jnp.float32, 0.0, 1.0)
    rate = jnp.exp(low + (high - low) * level)
    return -jnp.log(jnp.expm1(rate))


def strengthened(drawn, stream_key, source, target, blocks, factor):
    owner, partner = [(jnp.arange(drawn.shape[dim]) // (drawn.shape[dim] // blocks)).reshape([-1 if axis == dim else 1 for axis in range(drawn.ndim)]) for dim in (source, target)]
    chosen = jax.random.permutation(stream_key, blocks)[partner]
    strong = (owner == chosen) | (owner == (partner + blocks // 2) % blocks)
    return jnp.where(strong, factor * drawn, drawn)


def level_of(own_key, shape, shards, low, largest):
    factor_of = 1.0
    for position, blocks in shards:
        steps = jax.random.uniform(jax.random.fold_in(jax.random.fold_in(own_key, 6), position), (blocks,), jnp.float32, low / len(shards), largest / len(shards))
        factor_of = factor_of * jnp.repeat(jnp.exp(steps), shape[position] // blocks).reshape((-1,) + (1,) * (len(shape) - 1 - position))
    return factor_of


def noise(key, shape, spread, reach, split=(), kind=jnp.bfloat16):
    array = spread * jax.random.normal(key, shape, jnp.float32)
    if split:
        array = array * level_of(key, shape, split, -0.22, 0.18)
    return jnp.clip(array, -reach, reach).astype(kind)


def noise_with(stream_key, shape, spread, most, shards, heavy, kind=jnp.bfloat16):
    result = spread * jax.random.normal(stream_key, shape, jnp.float32)
    if shards:
        result = result * level_of(stream_key, shape, shards, -0.22, 0.18)
    return jnp.clip(strengthened(result, jax.random.fold_in(stream_key, 3), *heavy), -most, most).astype(kind)


def setup_inputs(seed: int = 0) -> dict:
    splits = jax.random.split(jax.random.key(seed), 9)
    return {
        "block_input": noise(splits[0], (DOCS, TOKENS, WIDTH), 1.0, 6.0, ((0, 4), (1, 128))),
        "state_cotangent": noise_with(splits[1], (DOCS, TOKENS, WIDTH), 1.0, 24.0, ((0, 4), (1, 128)), (1, 2, 128, 5.5)),
        "recur_weight": noise(splits[2], (WIDTH, BW), BW ** -0.5, 0.375, ((0, 128),)),
        "input_weight": noise(splits[3], (WIDTH, BW), BW ** -0.5, 0.375, ((0, 128),)),
        "gate_bias": noise(splits[4], (2, WIDTH), 1.0, 4.0, (), jnp.float32),
        "conv_taps": noise(splits[5], (TAPS, WIDTH), 0.5, 3.0, (), jnp.float32),
        "conv_bias": noise(splits[6], (WIDTH,), 0.5, 3.0, (), jnp.float32),
        "decay_param": draw_decay_param(jax.random.fold_in(splits[8], 71), 0),
    }


QFLOOR = 0.001

def one_block(xin, dstate, wr, wi, taps, cbias, brec, binp, lam):
    xf = xin.astype(jnp.float32)
    steps = xf.shape[0]
    chans = xf.shape[1]
    padded = jnp.concatenate([jnp.zeros((3, chans), jnp.float32), xf], axis=0)
    conv_f = cbias[None, :] + taps[0][None, :] * padded[3:3 + steps]
    for k in range(1, 4):
        conv_f = conv_f + taps[k][None, :] * padded[3 - k:3 - k + steps]
    conv_out = conv_f.astype(jnp.bfloat16)
    pre_r = jnp.dot(conv_out, wr, preferred_element_type=jnp.float32) + brec[None, :]
    pre_i = jnp.dot(conv_out, wi, preferred_element_type=jnp.float32) + binp[None, :]
    rgate = jax.nn.sigmoid(pre_r)
    igate = jax.nn.sigmoid(pre_i)
    rate = jax.nn.softplus(-lam)
    log_a = -8.0 * rgate * rate[None, :]
    decay = jnp.exp(log_a)
    qvalue = -jnp.expm1(2.0 * log_a)
    mult = jnp.sqrt(qvalue)
    conv_v = conv_out.astype(jnp.float32)
    normed = conv_v * igate * mult

    def fwd(state, pair):
        new_state = pair[0] * state + pair[1]
        return (new_state, new_state)
    zero_row = jnp.zeros((chans,), jnp.float32)
    _, hstates = lax.scan(fwd, zero_row, (decay, normed))
    h_prev = jnp.concatenate([zero_row[None, :], hstates[:-1]], axis=0)
    a_next = jnp.concatenate([decay[1:], zero_row[None, :]], axis=0)

    def bwd(carry, pair):
        new_carry = pair[1] + pair[0] * carry
        return (new_carry, new_carry)
    _, gvals = lax.scan(bwd, zero_row, (a_next, dstate.astype(jnp.float32)), reverse=True)
    grad_log_a = gvals * decay * h_prev - gvals * conv_v * igate * decay * decay / jnp.sqrt(jnp.maximum(qvalue, QFLOOR))
    gpr = (grad_log_a * (-8.0 * rate[None, :]) * rgate * (1.0 - rgate)).astype(jnp.bfloat16)
    gpi = (gvals * conv_v * mult * igate * (1.0 - igate)).astype(jnp.bfloat16)
    grad_conv = gvals * igate * mult
    grad_conv = grad_conv + jnp.dot(gpr, wr.T, preferred_element_type=jnp.float32)
    grad_conv = grad_conv + jnp.dot(gpi, wi.T, preferred_element_type=jnp.float32)
    dpad = jnp.concatenate([grad_conv, jnp.zeros((3, chans), jnp.float32)], axis=0)
    xgrad = taps[0][None, :] * dpad[0:steps]
    for k in range(1, 4):
        xgrad = xgrad + taps[k][None, :] * dpad[k:k + steps]
    xgrad = xgrad.astype(jnp.bfloat16)
    grad_r = jnp.dot(conv_out.T, gpr, preferred_element_type=jnp.float32)
    grad_i = jnp.dot(conv_out.T, gpi, preferred_element_type=jnp.float32)
    rows = [lax.optimization_barrier(jnp.sum(grad_conv * padded[3 - k:3 - k + steps], axis=0)) for k in range(4)]
    rows.append(lax.optimization_barrier(jnp.sum(grad_conv, axis=0)))
    rows.append(lax.optimization_barrier(jnp.sum(gpr.astype(jnp.float32), axis=0)))
    rows.append(lax.optimization_barrier(jnp.sum(gpi.astype(jnp.float32), axis=0)))
    rows.append(lax.optimization_barrier(jnp.sum(grad_log_a * 8.0 * rgate, axis=0)) * jax.nn.sigmoid(-lam))
    return (xgrad, grad_r, grad_i, jnp.stack(rows, axis=0))

def reference(block_input, state_cotangent, recur_weight, input_weight, gate_bias, conv_taps, conv_bias, decay_param):

    def run(index):
        dnum = (index // NB).astype(jnp.int32)
        bnum = (index % NB).astype(jnp.int32)
        col = (bnum * BW).astype(jnp.int32)
        zero = jnp.zeros((), jnp.int32)
        xin = lax.dynamic_slice(block_input, (dnum, zero, col), (1, TOKENS, BW))[0]
        dstate = lax.dynamic_slice(state_cotangent, (dnum, zero, col), (1, TOKENS, BW))[0]
        wr = lax.dynamic_slice(recur_weight, (col, zero), (BW, BW))
        wi = lax.dynamic_slice(input_weight, (col, zero), (BW, BW))
        taps = lax.dynamic_slice(conv_taps, (zero, col), (4, BW))
        cbias = lax.dynamic_slice(conv_bias, (col,), (BW,))
        brec = lax.dynamic_slice(gate_bias, (zero, col), (1, BW))[0]
        binp = lax.dynamic_slice(gate_bias, (zero + 1, col), (1, BW))[0]
        lam = lax.dynamic_slice(decay_param, (col,), (BW,))
        return one_block(xin, dstate, wr, wi, taps, cbias, brec, binp, lam)
    xgrad, grad_r, grad_i, chan = lax.map(run, jnp.arange(DOCS * NB, dtype=jnp.int32))
    input_grad = xgrad.reshape(DOCS, NB, TOKENS, BW).transpose(0, 2, 1, 3).reshape(DOCS, TOKENS, WIDTH)
    recur_weight_grad = lax.optimization_barrier(jnp.sum(grad_r.reshape(DOCS, NB, BW, BW), axis=0)).reshape(WIDTH, BW)
    input_weight_grad = lax.optimization_barrier(jnp.sum(grad_i.reshape(DOCS, NB, BW, BW), axis=0)).reshape(WIDTH, BW)
    channel_grads = lax.optimization_barrier(jnp.sum(chan.reshape(DOCS, NB, 8, BW), axis=0)).transpose(1, 0, 2).reshape(8, WIDTH)
    return (input_grad, recur_weight_grad, input_weight_grad, channel_grads)
```

```python
import functools

import jax
import jax.numpy as jnp
from jax import lax
from jax.experimental import pallas as pl
from jax.experimental.pallas import tpu as pltpu
from jax.sharding import Mesh
from jax.sharding import PartitionSpec as P

QFLOOR = 0.001
SEGS = 8
SPAN = 16
ROWS = SEGS * SPAN
F32 = jnp.float32
BF16 = jnp.bfloat16


def dot(a, b, contract=((1,), (0,))):
    return lax.dot_general(a, b, (contract, ((), ())), preferred_element_type=F32)


def shuffle_matrix():
    row = lax.broadcasted_iota(jnp.int32, (ROWS, ROWS), 0)
    col = lax.broadcasted_iota(jnp.int32, (ROWS, ROWS), 1)
    return jnp.where(col == (row % SEGS) * SPAN + row // SEGS, 1.0, 0.0).astype(BF16)


def by_step(buf_ref, shuffle, first):
    tiles = [buf_ref[s, pl.ds(first, SPAN), :] for s in range(SEGS)]
    return dot(shuffle, jnp.concatenate(tiles, axis=0))


def load_weights(buf_ref, w_ref, steps):
    block = w_ref.shape[0]
    share = block // 2 // SEGS
    for p in range(2):
        for s in range(SEGS):
            row = p * (block // 2) + s * share
            for w in range(2):
                at = 2 * steps + (p * 2 + w) * share
                w_ref[row : row + share, w * block : (w + 1) * block] = buf_ref[s, at : at + share, :]


def one_minus_exp(x):
    series = x * (1.0 - x * (1 / 2) * (1.0 - x * (1 / 3) * (1.0 - x * (1 / 4) * (1.0 - x * (1 / 5) * (1.0 - x * (1 / 6))))))
    return jnp.where(x < 0.25, series, 1.0 - jnp.exp(-x))


def block_params(at_ref, bias_ref, taps_ref, cbias_ref, decay_ref, block):
    lanes = pl.ds(pl.multiple_of(at_ref[1] * block, block), block)
    rate = jax.nn.softplus(-decay_ref[:, lanes])
    return bias_ref[:, lanes], taps_ref[:, lanes], cbias_ref[:, lanes], rate


def forward_kernel(
    steps, at_ref, buf_ref, halo_ref, bias_ref, taps_ref, cbias_ref, decay_ref,
    conv_ref, r_ref, i_ref, a_ref, m_ref, xpad_ref, seg_ref, sum_ref, w_ref,
):
    block = w_ref.shape[0]
    shuffle = shuffle_matrix()
    load_weights(buf_ref, w_ref, steps)
    bias, taps, cbias, rate = block_params(at_ref, bias_ref, taps_ref, cbias_ref, decay_ref, block)
    last = by_step(buf_ref, shuffle, steps - SPAN)[ROWS - 3 * SEGS :]
    halo = jnp.where(at_ref[0] > 0, halo_ref[...].astype(F32), 0.0)
    for k in range(3):
        rows = last[k * SEGS : (k + 1) * SEGS]
        xpad_ref[k * SEGS : (k + 1) * SEGS, :] = jnp.concatenate(
            [halo[SPAN - 3 + k : SPAN - 2 + k], rows[: SEGS - 1]], axis=0
        )

    def chunk(c, carry):
        prod, state, start = carry
        base = pl.multiple_of(c * ROWS, ROWS)
        first = pl.multiple_of(c * SPAN, SPAN)
        x = by_step(buf_ref, shuffle, first)
        d = by_step(buf_ref, shuffle, steps + first)
        xpad_ref[pl.ds(base + 3 * SEGS, ROWS), :] = x
        conv = cbias + taps[0:1] * x
        for k in range(1, 4):
            conv = conv + taps[k : k + 1] * xpad_ref[pl.ds(base + (3 - k) * SEGS, ROWS), :]
        conv_b = conv.astype(BF16)
        conv_ref[pl.ds(base, ROWS), :] = conv_b
        conv_v = conv_b.astype(F32)
        pre = dot(conv_b, w_ref[...])
        r = jax.nn.sigmoid(pre[:, :block] + bias[0:1])
        i = jax.nn.sigmoid(pre[:, block:] + bias[1:2])
        decay = 8.0 * r * rate
        a = jnp.exp(-decay)
        m = jnp.sqrt(one_minus_exp(2.0 * decay))
        r_ref[pl.ds(base, ROWS), :] = r
        i_ref[pl.ds(base, ROWS), :] = i
        a_ref[pl.ds(base, ROWS), :] = a
        m_ref[pl.ds(base, ROWS), :] = m
        normed = conv_v * i * m
        for s in range(SPAN):
            rows = slice(s * SEGS, (s + 1) * SEGS)
            prod = prod * a[rows]
            state = a[rows] * state + normed[rows]
            start = start + prod * d[rows]
        return prod, state, start

    zero = jnp.zeros((SEGS, block), F32)
    prod, state, start = lax.fori_loop(0, steps // SPAN, chunk, (zero + 1.0, zero, zero))
    seg_ref[0:SEGS, :] = prod
    seg_ref[SEGS : 2 * SEGS, :] = state
    seg_ref[2 * SEGS : 3 * SEGS, :] = start
    whole, end, begin = prod[0:1], state[0:1], start[SEGS - 1 : SEGS]
    for s in range(1, SEGS):
        whole = whole * prod[s : s + 1]
        end = prod[s : s + 1] * end + state[s : s + 1]
        back = SEGS - 1 - s
        begin = start[back : back + 1] + prod[back : back + 1] * begin
    sum_ref[...] = jnp.concatenate([whole, end, begin, begin], axis=0)


def backward_kernel(
    steps, shards, at_ref, buf_ref, conv_ref, r_ref, i_ref, a_ref, m_ref, xpad_ref, seg_ref, all_ref, w_ref,
    bias_ref, taps_ref, cbias_ref, decay_ref,
    ig_ref, wg_ref, rows_ref, edge_ref,
    prev_ref, gates_ref,
):
    block = w_ref.shape[0]
    shuffle = shuffle_matrix()
    _, taps, _, rate = block_params(at_ref, bias_ref, taps_ref, cbias_ref, decay_ref, block)
    mine = at_ref[0]
    entering = jnp.zeros((1, block), F32)
    carry_in = jnp.zeros((1, block), F32)
    for k in range(shards):
        part = all_ref[k]
        entering = jnp.where(k < mine, part[0:1] * entering + part[1:2], entering)
        back = shards - 1 - k
        part = all_ref[back]
        carry_in = jnp.where(back > mine, part[0:1] * carry_in + part[2:3], carry_in)
    heads, tails = [entering], [carry_in]
    for s in range(SEGS - 1):
        heads.append(seg_ref[s : s + 1] * heads[-1] + seg_ref[SEGS + s : SEGS + s + 1])
        back = SEGS - 1 - s
        tails.append(seg_ref[2 * SEGS + back : 2 * SEGS + back + 1] + seg_ref[back : back + 1] * tails[-1])
    state = jnp.concatenate(heads, axis=0)
    carry = jnp.concatenate(tails[::-1], axis=0)

    def ahead(c, state):
        base = pl.multiple_of(c * ROWS, ROWS)
        rows = pl.ds(base, ROWS)
        a = a_ref[rows, :]
        normed = conv_ref[rows, :].astype(F32) * i_ref[rows, :] * m_ref[rows, :]
        before = []
        for s in range(SPAN):
            at = slice(s * SEGS, (s + 1) * SEGS)
            before.append(state)
            state = a[at] * state + normed[at]
        prev_ref[rows, :] = jnp.concatenate(before, axis=0)
        return state

    lax.fori_loop(0, steps // SPAN, ahead, state)

    def put(first, xgrad):
        tiles = dot(shuffle, xgrad.astype(BF16), ((0,), (0,))).astype(BF16)
        for s in range(SEGS):
            ig_ref[s, pl.ds(first, SPAN), :] = tiles[s * SPAN : (s + 1) * SPAN]

    def folded(v):
        return jnp.sum(v.reshape(SPAN, SEGS, block), axis=0)

    def chunk(c, carry, after, totals):
        base = pl.multiple_of(c * ROWS, ROWS)
        first = pl.multiple_of(c * SPAN, SPAN)
        rows = pl.ds(base, ROWS)
        d = by_step(buf_ref, shuffle, steps + first)
        a = a_ref[rows, :]
        held = [None] * SPAN
        for s in range(SPAN - 1, -1, -1):
            at = slice(s * SEGS, (s + 1) * SEGS)
            held[s] = d[at] + carry
            carry = a[at] * held[s]
        g = jnp.concatenate(held, axis=0)
        r, i, m = r_ref[rows, :], i_ref[rows, :], m_ref[rows, :]
        conv_v = conv_ref[rows, :].astype(F32)
        gi = g * i
        ga = g * a
        gla = ga * prev_ref[rows, :] - gi * conv_v * a * a * lax.rsqrt(jnp.maximum(m * m, QFLOOR))
        glr = gla * 8.0 * r
        gpr = (glr * (r - 1.0) * rate).astype(BF16)
        gim = gi * m
        gpi = (gim * conv_v * (1.0 - i)).astype(BF16)
        both = jnp.concatenate([gpr, gpi], axis=1)
        gates_ref[rows, :] = both
        gc = gim + dot(both, w_ref[...], ((1,), (1,)))
        padded = jnp.concatenate([gc, after], axis=0)
        xgrad = taps[0:1] * gc
        for k in range(1, 4):
            xgrad = xgrad + taps[k : k + 1] * padded[k * SEGS : k * SEGS + ROWS]
        new = [folded(gc * xpad_ref[pl.ds(base + (3 - k) * SEGS, ROWS), :]) for k in range(4)]
        new += [folded(gc), folded(gpr.astype(F32)), folded(gpi.astype(F32)), folded(glr)]
        totals = tuple(t + n for t, n in zip(totals, new, strict=True))
        return carry, gc[: 3 * SEGS], totals, xgrad

    final = steps // SPAN - 1
    zero = jnp.zeros((SEGS, block), F32)
    carry, after, totals, ending = chunk(final, carry, jnp.zeros((3 * SEGS, block), F32), (zero,) * 8)

    def turn(k, held):
        c = final - 1 - k
        carry, after, totals = held
        carry, after, totals, xgrad = chunk(c, carry, after, totals)
        put(pl.multiple_of(c * SPAN, SPAN), xgrad)
        return carry, after, totals

    carry, after, totals = lax.fori_loop(0, final, turn, (carry, after, totals))
    none = jnp.zeros((1, block), F32)
    follow = [jnp.concatenate([after[k * SEGS + 1 : (k + 1) * SEGS], none], axis=0) for k in range(3)]
    cut = ROWS - 3 * SEGS
    late = [ending[cut + k * SEGS : cut + (k + 1) * SEGS] for k in range(3)]
    for k in range(3):
        for n in range(k + 1):
            late[k] = late[k] + taps[3 - k + n : 4 - k + n] * follow[n]
    put(final * SPAN, jnp.concatenate([ending[:cut]] + late, axis=0))
    edge_ref[...] = jnp.concatenate(
        [after[k * SEGS : k * SEGS + 1] for k in range(3)] + [none] + [v[SEGS - 1 :] for v in late] + [none], axis=0
    )
    scale = jax.nn.sigmoid(-decay_ref[:, pl.ds(pl.multiple_of(at_ref[1] * block, block), block)])
    sums = [jnp.sum(t, axis=0, keepdims=True) for t in totals]
    sums[7] = sums[7] * scale
    rows_ref[...] = jnp.concatenate(sums, axis=0)
    wg = dot(conv_ref[...], gates_ref[...], ((0,), (0,)))
    half = block // 2
    for s in range(SEGS):
        for w in range(2):
            for h in range(2):
                at = [p * half + s * 16 + h * 8 for p in range(2)]
                lanes = slice(w * block, (w + 1) * block)
                pair = jnp.concatenate([wg[k : k + 8, lanes] for k in at], axis=0)
                wg_ref[s * 4 + w * 2 + h] = pair.astype(BF16)


def split(v):
    high = v.astype(BF16)
    return high, (v - high.astype(F32)).astype(BF16)


def joined(high, low):
    return high.astype(F32) + low.astype(F32)


def per_device(
    shards, docs, block_input, state_cotangent, recur_weight, input_weight, gate_bias, conv_taps, conv_bias, decay_param
):
    steps, width = block_input.shape[1:]
    block = recur_weight.shape[1]
    share = recur_weight.shape[0]
    z, j = lax.axis_index("z"), lax.axis_index("j")
    at = jnp.stack([z, j]).astype(jnp.int32)
    params = (gate_bias, conv_taps, conv_bias[None], decay_param[None])

    weights = jnp.concatenate([recur_weight, input_weight], axis=0)
    weights = jnp.broadcast_to(weights[None], (shards, 2 * share, block))
    weights = lax.all_to_all(weights, "z", 0, 0).reshape(SEGS, 4 * share, block)
    by_block = [v[0].reshape(steps, SEGS, block).transpose(1, 0, 2) for v in (block_input, state_cotangent)]
    buf = lax.all_to_all(jnp.concatenate(by_block + [weights], axis=1), "j", 0, 0)
    halo = lax.ppermute(
        buf[SEGS - 1, steps - SPAN : steps], "z", [(k, k + 1) for k in range(shards - 1)]
    )

    total = SEGS * steps
    smem = pl.BlockSpec(memory_space=pltpu.SMEM)
    vmem = pl.BlockSpec(memory_space=pltpu.VMEM)
    shape = jax.ShapeDtypeStruct
    limit = pltpu.CompilerParams(vmem_limit_bytes=48 * 1024 * 1024)
    full = shape((total, block), F32)
    conv, r, i, a, m, xpad, seg, summary, w = pl.pallas_call(
        functools.partial(forward_kernel, steps),
        out_shape=(
            shape((total, block), BF16), full, full, full, full,
            shape((total + 3 * SEGS, block), F32), shape((3 * SEGS, block), F32),
            shape((4, block), F32), shape((block, 2 * block), BF16),
        ),
        in_specs=[smem] + [vmem] * 6,
        out_specs=(vmem,) * 9,
        compiler_params=limit,
        name="forward",
    )(at, buf, halo, *params)

    everyone = lax.all_to_all(jnp.broadcast_to(summary[None], (shards, 4, block)), "z", 0, 0)

    ig, wg, rows, edge = pl.pallas_call(
        functools.partial(backward_kernel, steps, shards),
        out_shape=(
            shape((SEGS, steps, block), BF16), shape((4 * SEGS, 16, block), BF16),
            shape((8, block), F32), shape((8, block), F32),
        ),
        in_specs=[smem] + [vmem] * 14,
        out_specs=(vmem,) * 4,
        scratch_shapes=[pltpu.VMEM((total, block), F32), pltpu.VMEM((total, 2 * block), BF16)],
        compiler_params=limit,
        name="backward",
    )(at, buf, conv, r, i, a, m, xpad, seg, everyone, w, *params)

    head = lax.ppermute(edge[0:3], "z", [(k + 1, k) for k in range(shards - 1)])
    taps = lax.dynamic_slice_in_dim(conv_taps, j * block, block, axis=1)
    late = []
    for k in range(3):
        row = edge[4 + k]
        for n in range(k + 1):
            row = row + taps[3 - k + n] * head[n]
        late.append(row)
    ig = ig.at[SEGS - 1, steps - 3 :].set(jnp.stack(late).astype(BF16))
    ig = lax.all_to_all(ig, "j", 0, 0)
    input_grad = ig.transpose(1, 0, 2).reshape(1, steps, width)

    quarter = block // docs
    pieces = split(rows.reshape(SEGS, docs, quarter).reshape(SEGS * docs, 1, quarter))
    packed = jnp.pad(jnp.concatenate(pieces, axis=2), ((0, 0), (0, 7), (0, block - 2 * quarter)))
    got = lax.all_to_all(jnp.concatenate([wg, packed], axis=1), ("j", "doc"), 0, 0)
    got = got.reshape(SEGS, docs, 24, block)
    wsum = jnp.sum(got[:, :, :16].astype(F32), axis=1).reshape(shards, 8, block)
    csum = jnp.sum(joined(got[:, :, 16, :quarter], got[:, :, 16, quarter : 2 * quarter]), axis=1)
    csum = jnp.broadcast_to(csum.reshape(1, 2, block), (shards, 2, block))
    got = lax.all_to_all(jnp.concatenate((wsum.astype(BF16),) + split(csum), axis=1), "z", 0, 0)
    wsum = jnp.sum(got[:, :8].astype(F32), axis=0)
    csum = jnp.sum(joined(got[:, 8:10], got[:, 10:12]), axis=0)
    send = jnp.broadcast_to(jnp.concatenate([wsum, csum], axis=0)[None], (SEGS * docs, 10, block))
    got = lax.all_to_all(send, ("j", "doc"), 0, 0).reshape(SEGS, docs, 10, block)
    wgrads = lax.dynamic_index_in_dim(got[:, :, :8], j, 0, keepdims=False).reshape(2, 2 * 8, block)
    channel_grads = got[:, :, 8:].reshape(SEGS, docs, SEGS, quarter).transpose(0, 2, 1, 3).reshape(8, width)
    return input_grad, wgrads[0], wgrads[1], channel_grads


def solution(mesh):
    seq, docs = mesh.shape["seq"], mesh.shape["doc"]
    shards = seq // SEGS
    fine = Mesh(mesh.devices.reshape(shards, SEGS, docs), ("z", "j", "doc"))
    tokens, rows = P("doc", ("z", "j"), None), P(("z", "j"), None)
    return jax.shard_map(
        functools.partial(per_device, shards, docs),
        mesh=fine,
        in_specs=(tokens, tokens, rows, rows, P(), P(), P(), P()),
        out_specs=(tokens, rows, rows, P()),
        check_vma=False,
    )
```

```python
import functools

import jax
import jax.numpy as jnp
from jax import lax
from jax.experimental import pallas as pl
from jax.experimental.pallas import tpu as pltpu
from jax.sharding import Mesh
from jax.sharding import PartitionSpec as P

QFLOOR = 0.001
SEGS = 8
SPAN = 16
ROWS = SEGS * SPAN
F32 = jnp.float32
BF16 = jnp.bfloat16


def dot(a, b, contract=((1,), (0,))):
    return lax.dot_general(a, b, (contract, ((), ())), preferred_element_type=F32)


def shuffle_matrix():
    row = lax.broadcasted_iota(jnp.int32, (ROWS, ROWS), 0)
    col = lax.broadcasted_iota(jnp.int32, (ROWS, ROWS), 1)
    return jnp.where(col == (row % SEGS) * SPAN + row // SEGS, 1.0, 0.0).astype(BF16)


def by_step(buf_ref, shuffle, first):
    tiles = [buf_ref[s, pl.ds(first, SPAN), :] for s in range(SEGS)]
    return dot(shuffle, jnp.concatenate(tiles, axis=0))


def load_weights(buf_ref, w_ref, first):
    block = w_ref.shape[0]
    for s in range(SEGS):
        for p in range(2):
            for w in range(2):
                row, at = p * (block // 2) + s * 16, first + (p * 2 + w) * 16
                w_ref[row : row + 16, w * block : (w + 1) * block] = buf_ref[s, at : at + 16, :]


def one_minus_exp(x):
    series = x * (1.0 - x * (1 / 2) * (1.0 - x * (1 / 3) * (1.0 - x * (1 / 4) * (1.0 - x * (1 / 5) * (1.0 - x * (1 / 6))))))
    return jnp.where(x < 0.25, series, 1.0 - jnp.exp(-x))


def block_params(at_ref, bias_ref, taps_ref, cbias_ref, decay_ref, block):
    lanes = pl.ds(pl.multiple_of(at_ref[1] * block, block), block)
    rate = jax.nn.softplus(-decay_ref[:, lanes])
    return bias_ref[:, lanes], taps_ref[:, lanes], cbias_ref[:, lanes], rate


def forward_kernel(
    steps, at_ref, buf_ref, bias_ref, taps_ref, cbias_ref, decay_ref,
    conv_ref, r_ref, i_ref, a_ref, m_ref, xpad_ref, seg_ref, sum_ref, w_ref,
):
    block = w_ref.shape[0]
    shuffle = shuffle_matrix()
    load_weights(buf_ref, w_ref, 2 * steps)
    bias, taps, cbias, rate = block_params(at_ref, bias_ref, taps_ref, cbias_ref, decay_ref, block)
    last = by_step(buf_ref, shuffle, steps - SPAN)[ROWS - 3 * SEGS :]
    halo = jnp.where(at_ref[0] > 0, buf_ref[SEGS - 1, 2 * steps + 64 : 2 * steps + 80, :].astype(F32), 0.0)
    for k in range(3):
        rows = last[k * SEGS : (k + 1) * SEGS]
        xpad_ref[k * SEGS : (k + 1) * SEGS, :] = jnp.concatenate(
            [halo[SPAN - 3 + k : SPAN - 2 + k], rows[: SEGS - 1]], axis=0
        )

    def chunk(c, carry):
        prod, state, start = carry
        base = pl.multiple_of(c * ROWS, ROWS)
        first = pl.multiple_of(c * SPAN, SPAN)
        x = by_step(buf_ref, shuffle, first)
        d = by_step(buf_ref, shuffle, steps + first)
        xpad_ref[pl.ds(base + 3 * SEGS, ROWS), :] = x
        conv = cbias + taps[0:1] * x
        for k in range(1, 4):
            conv = conv + taps[k : k + 1] * xpad_ref[pl.ds(base + (3 - k) * SEGS, ROWS), :]
        conv_b = conv.astype(BF16)
        conv_ref[pl.ds(base, ROWS), :] = conv_b
        conv_v = conv_b.astype(F32)
        pre = dot(conv_b, w_ref[...])
        r = jax.nn.sigmoid(pre[:, :block] + bias[0:1])
        i = jax.nn.sigmoid(pre[:, block:] + bias[1:2])
        decay = 8.0 * r * rate
        a = jnp.exp(-decay)
        m = jnp.sqrt(one_minus_exp(2.0 * decay))
        r_ref[pl.ds(base, ROWS), :] = r
        i_ref[pl.ds(base, ROWS), :] = i
        a_ref[pl.ds(base, ROWS), :] = a
        m_ref[pl.ds(base, ROWS), :] = m
        normed = conv_v * i * m
        for s in range(SPAN):
            rows = slice(s * SEGS, (s + 1) * SEGS)
            prod = prod * a[rows]
            state = a[rows] * state + normed[rows]
            start = start + prod * d[rows]
        return prod, state, start

    zero = jnp.zeros((SEGS, block), F32)
    prod, state, start = lax.fori_loop(0, steps // SPAN, chunk, (zero + 1.0, zero, zero))
    seg_ref[0:SEGS, :] = prod
    seg_ref[SEGS : 2 * SEGS, :] = state
    seg_ref[2 * SEGS : 3 * SEGS, :] = start
    whole, end, begin = prod[0:1], state[0:1], start[SEGS - 1 : SEGS]
    for s in range(1, SEGS):
        whole = whole * prod[s : s + 1]
        end = prod[s : s + 1] * end + state[s : s + 1]
        back = SEGS - 1 - s
        begin = start[back : back + 1] + prod[back : back + 1] * begin
    sum_ref[...] = jnp.concatenate([whole, end, begin, begin], axis=0)


def backward_kernel(
    steps, shards, at_ref, buf_ref, conv_ref, r_ref, i_ref, a_ref, m_ref, xpad_ref, seg_ref, all_ref, w_ref,
    bias_ref, taps_ref, cbias_ref, decay_ref,
    ig_ref, wg_ref, rows_ref, edge_ref,
    prev_ref, gates_ref,
):
    block = w_ref.shape[0]
    shuffle = shuffle_matrix()
    _, taps, _, rate = block_params(at_ref, bias_ref, taps_ref, cbias_ref, decay_ref, block)
    mine = at_ref[0]
    entering = jnp.zeros((1, block), F32)
    carry_in = jnp.zeros((1, block), F32)
    for k in range(shards):
        part = all_ref[k]
        entering = jnp.where(k < mine, part[0:1] * entering + part[1:2], entering)
        back = shards - 1 - k
        part = all_ref[back]
        carry_in = jnp.where(back > mine, part[0:1] * carry_in + part[2:3], carry_in)
    heads, tails = [entering], [carry_in]
    for s in range(SEGS - 1):
        heads.append(seg_ref[s : s + 1] * heads[-1] + seg_ref[SEGS + s : SEGS + s + 1])
        back = SEGS - 1 - s
        tails.append(seg_ref[2 * SEGS + back : 2 * SEGS + back + 1] + seg_ref[back : back + 1] * tails[-1])
    state = jnp.concatenate(heads, axis=0)
    carry = jnp.concatenate(tails[::-1], axis=0)

    def ahead(c, state):
        base = pl.multiple_of(c * ROWS, ROWS)
        rows = pl.ds(base, ROWS)
        a = a_ref[rows, :]
        normed = conv_ref[rows, :].astype(F32) * i_ref[rows, :] * m_ref[rows, :]
        before = []
        for s in range(SPAN):
            at = slice(s * SEGS, (s + 1) * SEGS)
            before.append(state)
            state = a[at] * state + normed[at]
        prev_ref[rows, :] = jnp.concatenate(before, axis=0)
        return state

    lax.fori_loop(0, steps // SPAN, ahead, state)

    def put(first, xgrad):
        tiles = dot(shuffle, xgrad.astype(BF16), ((0,), (0,))).astype(BF16)
        for s in range(SEGS):
            ig_ref[s, pl.ds(first, SPAN), :] = tiles[s * SPAN : (s + 1) * SPAN]

    def folded(v):
        return jnp.sum(v.reshape(SPAN, SEGS, block), axis=0)

    def chunk(c, carry, after, totals):
        base = pl.multiple_of(c * ROWS, ROWS)
        first = pl.multiple_of(c * SPAN, SPAN)
        rows = pl.ds(base, ROWS)
        d = by_step(buf_ref, shuffle, steps + first)
        a = a_ref[rows, :]
        held = [None] * SPAN
        for s in range(SPAN - 1, -1, -1):
            at = slice(s * SEGS, (s + 1) * SEGS)
            held[s] = d[at] + carry
            carry = a[at] * held[s]
        g = jnp.concatenate(held, axis=0)
        r, i, m = r_ref[rows, :], i_ref[rows, :], m_ref[rows, :]
        conv_v = conv_ref[rows, :].astype(F32)
        gi = g * i
        ga = g * a
        gla = ga * prev_ref[rows, :] - gi * conv_v * a * a * lax.rsqrt(jnp.maximum(m * m, QFLOOR))
        glr = gla * 8.0 * r
        gpr = (glr * (r - 1.0) * rate).astype(BF16)
        gim = gi * m
        gpi = (gim * conv_v * (1.0 - i)).astype(BF16)
        both = jnp.concatenate([gpr, gpi], axis=1)
        gates_ref[rows, :] = both
        gc = gim + dot(both, w_ref[...], ((1,), (1,)))
        padded = jnp.concatenate([gc, after], axis=0)
        xgrad = taps[0:1] * gc
        for k in range(1, 4):
            xgrad = xgrad + taps[k : k + 1] * padded[k * SEGS : k * SEGS + ROWS]
        new = [folded(gc * xpad_ref[pl.ds(base + (3 - k) * SEGS, ROWS), :]) for k in range(4)]
        new += [folded(gc), folded(gpr.astype(F32)), folded(gpi.astype(F32)), folded(glr)]
        totals = tuple(t + n for t, n in zip(totals, new, strict=True))
        return carry, gc[: 3 * SEGS], totals, xgrad

    final = steps // SPAN - 1
    zero = jnp.zeros((SEGS, block), F32)
    carry, after, totals, ending = chunk(final, carry, jnp.zeros((3 * SEGS, block), F32), (zero,) * 8)

    def turn(k, held):
        c = final - 1 - k
        carry, after, totals = held
        carry, after, totals, xgrad = chunk(c, carry, after, totals)
        put(pl.multiple_of(c * SPAN, SPAN), xgrad)
        return carry, after, totals

    carry, after, totals = lax.fori_loop(0, final, turn, (carry, after, totals))
    none = jnp.zeros((1, block), F32)
    follow = [jnp.concatenate([after[k * SEGS + 1 : (k + 1) * SEGS], none], axis=0) for k in range(3)]
    cut = ROWS - 3 * SEGS
    late = [ending[cut + k * SEGS : cut + (k + 1) * SEGS] for k in range(3)]
    for k in range(3):
        for n in range(k + 1):
            late[k] = late[k] + taps[3 - k + n : 4 - k + n] * follow[n]
    put(final * SPAN, jnp.concatenate([ending[:cut]] + late, axis=0))
    edge_ref[...] = jnp.concatenate(
        [after[k * SEGS : k * SEGS + 1] for k in range(3)] + [none] + [v[SEGS - 1 :] for v in late] + [none], axis=0
    )
    scale = jax.nn.sigmoid(-decay_ref[:, pl.ds(pl.multiple_of(at_ref[1] * block, block), block)])
    sums = [jnp.sum(t, axis=0, keepdims=True) for t in totals]
    sums[7] = sums[7] * scale
    rows_ref[...] = jnp.concatenate(sums, axis=0)
    wg = dot(conv_ref[...], gates_ref[...], ((0,), (0,)))
    for s in range(SEGS):
        for q in range(4):
            for p in range(2):
                row = p * (block // 2) + s * 16
                tile = wg[row : row + 16, q * 128 : (q + 1) * 128]
                wg_ref[s * 4 + q, p * 16 : (p + 1) * 16, :] = tile.astype(BF16)


def unpack_kernel(steps, got_ref, ig_ref, rows_ref):
    block = got_ref.shape[2]
    for b in range(SEGS):
        ig_ref[0, :, b * block : (b + 1) * block] = got_ref[b, :steps, :]
        pair = got_ref[b, steps : steps + 2 * SEGS, :].astype(F32)
        row = pair[:SEGS] + pair[SEGS:]
        for k in range(SEGS):
            rows_ref[b : b + 1, k * block : (k + 1) * block] = row[k : k + 1]


def split(v):
    high = v.astype(BF16)
    return high, (v - high.astype(F32)).astype(BF16)


def joined(high, low):
    return high.astype(F32) + low.astype(F32)


def per_device(
    shards, docs, block_input, state_cotangent, recur_weight, input_weight, gate_bias, conv_taps, conv_bias, decay_param
):
    steps, width = block_input.shape[1:]
    block = recur_weight.shape[1]
    share = recur_weight.shape[0]
    z, j = lax.axis_index("z"), lax.axis_index("j")
    at = jnp.stack([z, j]).astype(jnp.int32)
    params = (gate_bias, conv_taps, conv_bias[None], decay_param[None])

    weights = jnp.concatenate([recur_weight, input_weight], axis=0)
    weights = jnp.broadcast_to(weights[None], (shards, 2 * share, block))
    weights = lax.all_to_all(weights, "z", 0, 0).reshape(SEGS, 4 * share, block)
    forth = [(k, k + 1) for k in range(shards - 1)]
    halo = lax.ppermute(block_input[0, steps - 16 :], "z", forth)
    tokens = (block_input[0], state_cotangent[0], halo)
    xs, ds, halo = (v.reshape(-1, SEGS, block).transpose(1, 0, 2) for v in tokens)
    buf = lax.all_to_all(jnp.concatenate([xs, ds, weights, halo], axis=1), "j", 0, 0)

    total = SEGS * steps
    smem = pl.BlockSpec(memory_space=pltpu.SMEM)
    vmem = pl.BlockSpec(memory_space=pltpu.VMEM)
    shape = jax.ShapeDtypeStruct
    limit = pltpu.CompilerParams(vmem_limit_bytes=24 * 1024 * 1024)
    full = shape((total, block), F32)
    conv, r, i, a, m, xpad, seg, summary, w = pl.pallas_call(
        functools.partial(forward_kernel, steps),
        out_shape=(
            shape((total, block), BF16), full, full, full, full,
            shape((total + 3 * SEGS, block), F32), shape((3 * SEGS, block), F32),
            shape((4, block), F32), shape((block, 2 * block), BF16),
        ),
        in_specs=[smem] + [vmem] * 5,
        out_specs=(vmem,) * 9,
        compiler_params=limit,
        name="forward",
    )(at, buf, *params)

    everyone = lax.all_to_all(jnp.broadcast_to(summary[None], (shards, 4, block)), "z", 0, 0)

    ig, wg, rows, edge = pl.pallas_call(
        functools.partial(backward_kernel, steps, shards),
        out_shape=(
            shape((SEGS, steps, block), BF16), shape((4 * SEGS, 32, 128), BF16),
            shape((8, block), F32), shape((8, block), F32),
        ),
        in_specs=[smem] + [vmem] * 14,
        out_specs=(vmem,) * 4,
        scratch_shapes=[pltpu.VMEM((total, block), F32), pltpu.VMEM((total, 2 * block), BF16)],
        compiler_params=limit,
        name="backward",
    )(at, buf, conv, r, i, a, m, xpad, seg, everyone, w, *params)

    head = lax.ppermute(edge[0:3], "z", [(k + 1, k) for k in range(shards - 1)])
    taps = lax.dynamic_slice_in_dim(conv_taps, j * block, block, axis=1)
    late = []
    for k in range(3):
        row = edge[4 + k]
        for n in range(k + 1):
            row = row + taps[3 - k + n] * head[n]
        late.append(row)
    ig = ig.at[SEGS - 1, steps - 3 :].set(jnp.stack(late).astype(BF16))
    quarter = block // docs
    packed = jnp.concatenate(split(rows.reshape(SEGS * docs, 1, quarter)), axis=2)
    got = lax.all_to_all(jnp.concatenate([wg, packed], axis=1), ("j", "doc"), 0, 0)
    got = got.reshape(SEGS, docs, 33, 128)
    wsum = jnp.sum(got[:, :, :32].astype(F32), axis=1).reshape(shards, 16, 128)
    csum = jnp.sum(joined(got[:, :, 32, :quarter], got[:, :, 32, quarter:]), axis=1)
    csum = jnp.broadcast_to(csum.reshape(1, 4, 128), (shards, 4, 128))
    got = lax.all_to_all(jnp.concatenate((wsum.astype(BF16),) + split(csum), axis=1), "z", 0, 0)
    wsum = jnp.sum(got[:, :16].astype(F32), axis=0)
    csum = jnp.sum(joined(got[:, 16:20], got[:, 20:]), axis=0)
    send = jnp.concatenate([wsum, csum], axis=0)
    got = lax.all_to_all(jnp.broadcast_to(send[None], (docs, 20, 128)), "doc", 0, 0)
    wgrads = got[:, :16].reshape(2, 2, 16, 128).transpose(0, 2, 1, 3).reshape(2, 16, block)
    csum = got[:, 16:].reshape(docs, SEGS, quarter).transpose(1, 0, 2).reshape(SEGS, block)
    csum = jnp.broadcast_to(jnp.concatenate(split(csum), axis=0)[None], (SEGS, 2 * SEGS, block))
    got = lax.all_to_all(jnp.concatenate([ig, csum], axis=1), "j", 0, 0)
    input_grad, channel_grads = pl.pallas_call(
        functools.partial(unpack_kernel, steps),
        out_shape=(shape((1, steps, width), BF16), shape((SEGS, width), F32)),
        in_specs=[vmem],
        out_specs=(vmem,) * 2,
        compiler_params=limit,
        name="unpack",
    )(got)
    return input_grad, wgrads[0], wgrads[1], channel_grads


def solution(mesh):
    seq, docs = mesh.shape["seq"], mesh.shape["doc"]
    shards = seq // SEGS
    fine = Mesh(mesh.devices.reshape(shards, SEGS, docs), ("z", "j", "doc"))
    tokens, rows = P("doc", ("z", "j"), None), P(("z", "j"), None)
    return jax.shard_map(
        functools.partial(per_device, shards, docs),
        mesh=fine,
        in_specs=(tokens, tokens, rows, rows, P(), P(), P(), P()),
        out_specs=(tokens, rows, rows, P()),
        check_vma=False,
    )
```

```python
import functools

import jax
import jax.numpy as jnp
from jax import lax
from jax.experimental import pallas as pl
from jax.experimental.pallas import tpu as pltpu
from jax.sharding import Mesh
from jax.sharding import PartitionSpec as P

QFLOOR = 0.001
SEGS = 8
SPAN = 16
ROWS = SEGS * SPAN
UNROLL = (True, True, True, True)
F32 = jnp.float32
BF16 = jnp.bfloat16


def dot(a, b, contract=((1,), (0,))):
    return lax.dot_general(a, b, (contract, ((), ())), preferred_element_type=F32)


def shuffle_matrix():
    row = lax.broadcasted_iota(jnp.int32, (ROWS, ROWS), 0)
    col = lax.broadcasted_iota(jnp.int32, (ROWS, ROWS), 1)
    return jnp.where(col == (row % SEGS) * SPAN + row // SEGS, 1.0, 0.0).astype(BF16)


def by_step(buf_ref, shuffle, first):
    tiles = [buf_ref[s, pl.ds(first, SPAN), :] for s in range(SEGS)]
    return dot(shuffle, jnp.concatenate(tiles, axis=0))


def load_weights(buf_ref, w_ref, first):
    block = w_ref.shape[0]
    for s in range(SEGS):
        for p in range(2):
            for w in range(2):
                row, at = p * (block // 2) + s * 16, first + (p * 2 + w) * 16
                w_ref[row : row + 16, w * block : (w + 1) * block] = buf_ref[s, at : at + 16, :]


def one_minus_square(a, decay):
    x = 2.0 * decay
    series = x * (1.0 - x * (1 / 2) * (1.0 - x * (1 / 3) * (1.0 - x * (1 / 4))))
    return jnp.where(x < 0.0625, series, 1.0 - a * a)


def sigmoid(x):
    below = 1.0 + jnp.exp(-jnp.maximum(x, -80.0))
    guess = pl.reciprocal(below, approx=True)
    return guess * (2.0 - below * guess)


def block_params(at_ref, bias_ref, taps_ref, cbias_ref, decay_ref, block):
    lanes = pl.ds(pl.multiple_of(at_ref[1] * block, block), block)
    rate = jax.nn.softplus(-decay_ref[:, lanes])
    return bias_ref[:, lanes], taps_ref[:, lanes], cbias_ref[:, lanes], rate


def forward_kernel(
    steps, at_ref, buf_ref, bias_ref, taps_ref, cbias_ref, decay_ref,
    conv_ref, r_ref, i_ref, a_ref, m_ref, xpad_ref, seg_ref, sum_ref, w_ref,
):
    block = w_ref.shape[0]
    shuffle = shuffle_matrix()
    load_weights(buf_ref, w_ref, 2 * steps)
    bias, taps, cbias, rate = block_params(at_ref, bias_ref, taps_ref, cbias_ref, decay_ref, block)
    rate8 = 8.0 * rate
    last = by_step(buf_ref, shuffle, steps - SPAN)[ROWS - 3 * SEGS :]
    halo = jnp.where(at_ref[0] > 0, buf_ref[SEGS - 1, 2 * steps + 64 : 2 * steps + 80, :].astype(F32), 0.0)
    for k in range(3):
        rows = last[k * SEGS : (k + 1) * SEGS]
        xpad_ref[k * SEGS : (k + 1) * SEGS, :] = jnp.concatenate(
            [halo[k : k + 1], rows[: SEGS - 1]], axis=0
        )

    def chunk(c, carry):
        prod, state, start = carry
        base = pl.multiple_of(c * ROWS, ROWS)
        first = pl.multiple_of(c * SPAN, SPAN)
        x = by_step(buf_ref, shuffle, first)
        d = by_step(buf_ref, shuffle, steps + first)
        xpad_ref[pl.ds(base + 3 * SEGS, ROWS), :] = x
        conv = cbias + taps[0:1] * x
        for k in range(1, 4):
            conv = conv + taps[k : k + 1] * xpad_ref[pl.ds(base + (3 - k) * SEGS, ROWS), :]
        conv_b = conv.astype(BF16)
        conv_ref[pl.ds(base, ROWS), :] = conv_b
        conv_v = conv_b.astype(F32)
        pre = dot(conv_b, w_ref[...])
        r = sigmoid(pre[:, :block] + bias[0:1])
        i = sigmoid(pre[:, block:] + bias[1:2])
        decay = r * rate8
        a = jnp.exp(-decay)
        q = one_minus_square(a, decay)
        m = q * lax.rsqrt(jnp.maximum(q, 1e-37))
        r_ref[pl.ds(base, ROWS), :] = r
        i_ref[pl.ds(base, ROWS), :] = i
        a_ref[pl.ds(base, ROWS), :] = a
        m_ref[pl.ds(base, ROWS), :] = m
        normed = conv_v * i * m
        for s in range(SPAN):
            rows = slice(s * SEGS, (s + 1) * SEGS)
            prod = prod * a[rows]
            state = a[rows] * state + normed[rows]
            start = start + prod * d[rows]
        return prod, state, start

    zero = jnp.zeros((SEGS, block), F32)
    prod, state, start = lax.fori_loop(0, steps // SPAN, chunk, (zero + 1.0, zero, zero), unroll=UNROLL[0])
    seg_ref[0:SEGS, :] = prod
    seg_ref[SEGS : 2 * SEGS, :] = state
    seg_ref[2 * SEGS : 3 * SEGS, :] = start
    whole, end, begin = prod[0:1], state[0:1], start[SEGS - 1 : SEGS]
    for s in range(1, SEGS):
        whole = whole * prod[s : s + 1]
        end = prod[s : s + 1] * end + state[s : s + 1]
        back = SEGS - 1 - s
        begin = start[back : back + 1] + prod[back : back + 1] * begin
    summary = jnp.concatenate([whole, end, begin, begin], axis=0)
    for k in range(sum_ref.shape[0]):
        sum_ref[k] = summary


def backward_kernel(
    steps, shards, at_ref, buf_ref, all_ref, seg_ref, conv_ref, r_ref, i_ref, a_ref, m_ref, xpad_ref, w_ref, decay_ref,
    gc_ref, wg_ref, rows_ref,
    prev_ref, gates_ref,
):
    block = w_ref.shape[0]
    shuffle = shuffle_matrix()
    mine = at_ref[0]
    decay = decay_ref[:, pl.ds(pl.multiple_of(at_ref[1] * block, block), block)]
    rate = jax.nn.softplus(-decay)
    entering = jnp.zeros((1, block), F32)
    carry_in = jnp.zeros((1, block), F32)
    for k in range(shards):
        part = all_ref[k]
        entering = jnp.where(k < mine, part[0:1] * entering + part[1:2], entering)
        back = shards - 1 - k
        part = all_ref[back]
        carry_in = jnp.where(back > mine, part[0:1] * carry_in + part[2:3], carry_in)
    heads, tails = [entering], [carry_in]
    for s in range(SEGS - 1):
        heads.append(seg_ref[s : s + 1] * heads[-1] + seg_ref[SEGS + s : SEGS + s + 1])
        back = SEGS - 1 - s
        tails.append(seg_ref[2 * SEGS + back : 2 * SEGS + back + 1] + seg_ref[back : back + 1] * tails[-1])
    state = jnp.concatenate(heads, axis=0)
    carry = jnp.concatenate(tails[::-1], axis=0)

    def ahead(c, state):
        rows = pl.ds(pl.multiple_of(c * ROWS, ROWS), ROWS)
        a, m = a_ref[rows, :], m_ref[rows, :]
        ci = conv_ref[rows, :].astype(F32) * i_ref[rows, :]
        normed = ci * m
        before = []
        for s in range(SPAN):
            at = slice(s * SEGS, (s + 1) * SEGS)
            before.append(state)
            state = a[at] * state + normed[at]
        direct = ci * a * lax.rsqrt(jnp.maximum(m * m, QFLOOR))
        prev_ref[rows, :] = a * (jnp.concatenate(before, axis=0) - direct)
        return state

    lax.fori_loop(0, steps // SPAN, ahead, state, unroll=UNROLL[1])

    def folded(v):
        return jnp.sum(v.reshape(SPAN, SEGS, block), axis=0)

    def back(k, held):
        carry, totals = held
        c = steps // SPAN - 1 - k
        base = pl.multiple_of(c * ROWS, ROWS)
        rows = pl.ds(base, ROWS)
        d = by_step(buf_ref, shuffle, steps + pl.multiple_of(c * SPAN, SPAN))
        a = a_ref[rows, :]
        grads = [None] * SPAN
        for s in range(SPAN - 1, -1, -1):
            at = slice(s * SEGS, (s + 1) * SEGS)
            grads[s] = d[at] + carry
            carry = a[at] * grads[s]
        g = jnp.concatenate(grads, axis=0)
        r, i = r_ref[rows, :], i_ref[rows, :]
        glr = g * prev_ref[rows, :] * (8.0 * r)
        gpr = (glr * ((r - 1.0) * rate)).astype(BF16)
        gim = g * (i * m_ref[rows, :])
        gpi = (gim * (conv_ref[rows, :].astype(F32) * (1.0 - i))).astype(BF16)
        both = jnp.concatenate([gpr, gpi], axis=1)
        gates_ref[rows, :] = both
        gc = gim + dot(both, w_ref[...], ((1,), (1,)))
        gc_ref[rows, :] = gc
        new = [folded(gc * xpad_ref[pl.ds(base + (3 - k) * SEGS, ROWS), :]) for k in range(4)]
        new += [folded(gc), folded(gpr.astype(F32)), folded(gpi.astype(F32)), folded(glr)]
        return carry, tuple(t + n for t, n in zip(totals, new, strict=True))

    zero = jnp.zeros((SEGS, block), F32)
    _, totals = lax.fori_loop(0, steps // SPAN, back, (carry, (zero,) * 8), unroll=UNROLL[2])
    sums = [jnp.sum(t, axis=0, keepdims=True) for t in totals]
    sums[7] = sums[7] * jax.nn.sigmoid(-decay)
    rows_ref[...] = jnp.concatenate(sums, axis=0)
    wg = dot(conv_ref[...], gates_ref[...], ((0,), (0,)))
    for s in range(SEGS):
        for q in range(4):
            for p in range(2):
                row = p * (block // 2) + s * 16
                tile = wg[row : row + 16, q * 128 : (q + 1) * 128]
                wg_ref[s * 4 + q, p * 16 : (p + 1) * 16, :] = tile.astype(BF16)


def taps_kernel(steps, at_ref, gc_ref, head_ref, taps_ref, ig_ref, tail_ref):
    block = gc_ref.shape[1]
    shuffle = shuffle_matrix()
    taps = taps_ref[:, pl.ds(pl.multiple_of(at_ref[1] * block, block), block)]
    final = steps // SPAN - 1
    tail_ref[:ROWS, :] = gc_ref[final * ROWS :, :]
    for k in range(3):
        rows = gc_ref[k * SEGS + 1 : (k + 1) * SEGS, :]
        tail_ref[ROWS + k * SEGS : ROWS + (k + 1) * SEGS, :] = jnp.concatenate([rows, head_ref[k : k + 1, :]], axis=0)

    def put(ref, base, first):
        xgrad = taps[0:1] * ref[pl.ds(base, ROWS), :]
        for k in range(1, 4):
            xgrad = xgrad + taps[k : k + 1] * ref[pl.ds(base + k * SEGS, ROWS), :]
        tiles = dot(shuffle, xgrad.astype(BF16), ((0,), (0,))).astype(BF16)
        for s in range(SEGS):
            ig_ref[s, pl.ds(first, SPAN), :] = tiles[s * SPAN : (s + 1) * SPAN]

    def turn(c, _):
        put(gc_ref, pl.multiple_of(c * ROWS, ROWS), pl.multiple_of(c * SPAN, SPAN))
        return 0

    lax.fori_loop(0, final, turn, 0, unroll=UNROLL[3])
    put(tail_ref, 0, final * SPAN)


def unpack_kernel(steps, got_ref, ig_ref, rows_ref):
    block = got_ref.shape[2]
    for b in range(SEGS):
        ig_ref[0, :, b * block : (b + 1) * block] = got_ref[b, :steps, :]
        pair = got_ref[b, steps : steps + 2 * SEGS, :].astype(F32)
        row = pair[:SEGS] + pair[SEGS:]
        for k in range(SEGS):
            rows_ref[b : b + 1, k * block : (k + 1) * block] = row[k : k + 1]


def split(v):
    high = lax.reduce_precision(v, 8, 7)
    return high.astype(BF16), (v - high).astype(BF16)


def joined(high, low):
    return high.astype(F32) + low.astype(F32)


def per_device(
    shards, docs, block_input, state_cotangent, recur_weight, input_weight, gate_bias, conv_taps, conv_bias, decay_param
):
    steps, width = block_input.shape[1:]
    block = recur_weight.shape[1]
    share = recur_weight.shape[0]
    z, j = lax.axis_index("z"), lax.axis_index("j")
    at = jnp.stack([z, j]).astype(jnp.int32)
    params = (gate_bias, conv_taps, conv_bias[None], decay_param[None])

    weights = jnp.concatenate([recur_weight, input_weight], axis=0)
    weights = jnp.broadcast_to(weights[None], (shards, 2 * share, block))
    weights = lax.all_to_all(weights, "z", 0, 0).reshape(SEGS, 4 * share, block)
    halo = lax.ppermute(block_input[0, steps - 3 :], "z", [(k, k + 1) for k in range(shards - 1)])
    halo = jnp.pad(halo, ((0, 13), (0, 0)))
    tokens = (block_input[0], state_cotangent[0], halo)
    xs, ds, halo = (v.reshape(-1, SEGS, block).transpose(1, 0, 2) for v in tokens)
    buf = lax.all_to_all(jnp.concatenate([xs, ds, weights, halo], axis=1), "j", 0, 0)

    total = SEGS * steps
    smem = pl.BlockSpec(memory_space=pltpu.SMEM)
    vmem = pl.BlockSpec(memory_space=pltpu.VMEM)
    shape = jax.ShapeDtypeStruct
    limit = pltpu.CompilerParams(vmem_limit_bytes=12 * 1024 * 1024)
    cost = pl.CostEstimate(flops=200 * total * block, bytes_accessed=12 * total * block, transcendentals=0)
    full, half = pltpu.VMEM((total, block), F32), pltpu.VMEM((total, block), BF16)

    def call(kernel, name, out_shape, operands, scratch=()):
        return pl.pallas_call(
            kernel,
            out_shape=out_shape,
            in_specs=[smem] + [vmem] * (len(operands) - 1),
            out_specs=(vmem,) * len(out_shape),
            scratch_shapes=scratch,
            compiler_params=limit,
            cost_estimate=cost,
            name=name,
        )(*operands)

    conv, r, i, a, m, xpad, seg, summary, w = call(
        functools.partial(forward_kernel, steps),
        "forward",
        (half, full, full, full, full, pltpu.VMEM((total + 3 * SEGS, block), F32), shape((3 * SEGS, block), F32))
        + (shape((shards, 4, block), F32), shape((block, 2 * block), BF16)),
        (at, buf, *params),
    )
    everyone = lax.all_to_all(summary, "z", 0, 0)
    gc, wg, rows = call(
        functools.partial(backward_kernel, steps, shards),
        "backward",
        (full, shape((4 * SEGS, 32, 128), BF16), shape((8, block), F32)),
        (at, buf, everyone, seg, conv, r, i, a, m, xpad, w, params[3]),
        [pltpu.VMEM((total, block), F32), pltpu.VMEM((total, 2 * block), BF16)],
    )
    head = gc[: 3 * SEGS].reshape(3, SEGS, block)[:, 0]
    head = lax.ppermute(head, "z", [(k + 1, k) for k in range(shards - 1)])
    (ig,) = call(
        functools.partial(taps_kernel, steps),
        "taps",
        (shape((SEGS, steps, block), BF16),),
        (at, gc, head, conv_taps),
        [pltpu.VMEM((ROWS + 3 * SEGS, block), F32)],
    )

    quarter = block // docs
    packed = jnp.concatenate(split(rows.reshape(SEGS * docs, 1, quarter)), axis=2)
    got = lax.all_to_all(jnp.concatenate([wg, packed], axis=1), ("j", "doc"), 0, 0)
    got = got.reshape(SEGS, docs, 33, 128)
    wsum = jnp.sum(got[:, :, :32].astype(F32), axis=1).reshape(shards, 16, 128)
    csum = jnp.sum(joined(got[:, :, 32, :quarter], got[:, :, 32, quarter:]), axis=1)
    csum = jnp.broadcast_to(csum.reshape(1, 4, 128), (shards, 4, 128))
    got = lax.all_to_all(jnp.concatenate((wsum.astype(BF16),) + split(csum), axis=1), "z", 0, 0)
    wsum = jnp.sum(got[:, :16].astype(F32), axis=0)
    csum = jnp.sum(joined(got[:, 16:20], got[:, 20:]), axis=0)
    send, ig = lax.optimization_barrier((jnp.concatenate([wsum, csum], axis=0), ig))
    got = lax.all_to_all(jnp.broadcast_to(send[None], (docs, 20, 128)), "doc", 0, 0)
    wgrads = got[:, :16].reshape(2, 2, 16, 128).transpose(0, 2, 1, 3).reshape(2, 16, block)
    csum = got[:, 16:].reshape(docs, SEGS, quarter).transpose(1, 0, 2).reshape(SEGS, block)
    csum = jnp.broadcast_to(jnp.concatenate(split(csum), axis=0)[None], (SEGS, 2 * SEGS, block))
    got = lax.all_to_all(jnp.concatenate([ig, csum], axis=1), "j", 0, 0)
    input_grad, channel_grads = pl.pallas_call(
        functools.partial(unpack_kernel, steps),
        out_shape=(shape((1, steps, width), BF16), shape((SEGS, width), F32)),
        in_specs=[vmem],
        out_specs=(vmem,) * 2,
        compiler_params=limit,
        name="unpack",
    )(got)
    return input_grad, wgrads[0], wgrads[1], channel_grads


def solution(mesh):
    seq, docs = mesh.shape["seq"], mesh.shape["doc"]
    shards = seq // SEGS
    fine = Mesh(mesh.devices.reshape(shards, SEGS, docs), ("z", "j", "doc"))
    tokens, rows = P("doc", ("z", "j"), None), P(("z", "j"), None)
    return jax.shard_map(
        functools.partial(per_device, shards, docs),
        mesh=fine,
        in_specs=(tokens, tokens, rows, rows, P(), P(), P(), P()),
        out_specs=(tokens, rows, rows, P()),
        check_vma=False,
    )
```

```python
import functools

import jax
import jax.numpy as jnp
from jax import lax
from jax.experimental import pallas as pl
from jax.experimental.pallas import tpu as pltpu
from jax.sharding import Mesh
from jax.sharding import PartitionSpec as P

QFLOOR = 0.001
SEGS = 8
SPAN = 16
ROWS = SEGS * SPAN
UNROLL = (True, True, True, True)
F32 = jnp.float32
BF16 = jnp.bfloat16


def dot(a, b, contract=((1,), (0,))):
    return lax.dot_general(a, b, (contract, ((), ())), preferred_element_type=F32)


def shuffle_matrix():
    row = lax.broadcasted_iota(jnp.int32, (ROWS, ROWS), 0)
    col = lax.broadcasted_iota(jnp.int32, (ROWS, ROWS), 1)
    return jnp.where(col == (row % SEGS) * SPAN + row // SEGS, 1.0, 0.0).astype(BF16)


def by_step(buf_ref, shuffle, first):
    tiles = [buf_ref[s, pl.ds(first, SPAN), :] for s in range(SEGS)]
    return dot(shuffle, jnp.concatenate(tiles, axis=0))


def load_weights(buf_ref, w_ref, first):
    block = w_ref.shape[0]
    for s in range(SEGS):
        for p in range(2):
            for w in range(2):
                row, at = p * (block // 2) + s * 16, first + (p * 2 + w) * 16
                w_ref[row : row + 16, w * block : (w + 1) * block] = buf_ref[s, at : at + 16, :]


def one_minus_square(a, decay):
    x = 2.0 * decay
    series = x * (1.0 - x * (1 / 2) * (1.0 - x * (1 / 3) * (1.0 - x * (1 / 4))))
    return jnp.where(x < 0.0625, series, 1.0 - a * a)


def sigmoid(x):
    below = 1.0 + jnp.exp(-jnp.maximum(x, -80.0))
    guess = pl.reciprocal(below, approx=True)
    return guess * (2.0 - below * guess)


def block_params(at_ref, bias_ref, taps_ref, cbias_ref, decay_ref, block):
    lanes = pl.ds(pl.multiple_of(at_ref[1] * block, block), block)
    rate = jax.nn.softplus(-decay_ref[:, lanes])
    return bias_ref[:, lanes], taps_ref[:, lanes], cbias_ref[:, lanes], rate


def forward_kernel(
    steps, at_ref, buf_ref, bias_ref, taps_ref, cbias_ref, decay_ref,
    conv_ref, r_ref, i_ref, a_ref, m_ref, xpad_ref, seg_ref, sum_ref, w_ref,
):
    block = w_ref.shape[0]
    shuffle = shuffle_matrix()
    load_weights(buf_ref, w_ref, 2 * steps)
    bias, taps, cbias, rate = block_params(at_ref, bias_ref, taps_ref, cbias_ref, decay_ref, block)
    rate8 = 8.0 * rate
    last = by_step(buf_ref, shuffle, steps - SPAN)[ROWS - 3 * SEGS :]
    halo = jnp.where(at_ref[0] > 0, buf_ref[SEGS - 1, 2 * steps + 64 : 2 * steps + 80, :].astype(F32), 0.0)
    for k in range(3):
        rows = last[k * SEGS : (k + 1) * SEGS]
        xpad_ref[k * SEGS : (k + 1) * SEGS, :] = jnp.concatenate(
            [halo[k : k + 1], rows[: SEGS - 1]], axis=0
        )

    def chunk(c, carry):
        prod, state, start = carry
        base = pl.multiple_of(c * ROWS, ROWS)
        first = pl.multiple_of(c * SPAN, SPAN)
        x = by_step(buf_ref, shuffle, first)
        d = by_step(buf_ref, shuffle, steps + first)
        xpad_ref[pl.ds(base + 3 * SEGS, ROWS), :] = x
        conv = cbias + taps[0:1] * x
        for k in range(1, 4):
            conv = conv + taps[k : k + 1] * xpad_ref[pl.ds(base + (3 - k) * SEGS, ROWS), :]
        conv_b = conv.astype(BF16)
        conv_ref[pl.ds(base, ROWS), :] = conv_b
        conv_v = conv_b.astype(F32)
        pre = dot(conv_b, w_ref[...])
        r = sigmoid(pre[:, :block] + bias[0:1])
        i = sigmoid(pre[:, block:] + bias[1:2])
        decay = r * rate8
        a = jnp.exp(-decay)
        q = one_minus_square(a, decay)
        m = q * lax.rsqrt(jnp.maximum(q, 1e-37))
        r_ref[pl.ds(base, ROWS), :] = r
        i_ref[pl.ds(base, ROWS), :] = i
        a_ref[pl.ds(base, ROWS), :] = a
        m_ref[pl.ds(base, ROWS), :] = m
        normed = conv_v * i * m
        for s in range(SPAN):
            rows = slice(s * SEGS, (s + 1) * SEGS)
            prod = prod * a[rows]
            state = a[rows] * state + normed[rows]
            start = start + prod * d[rows]
        return prod, state, start

    zero = jnp.zeros((SEGS, block), F32)
    prod, state, start = lax.fori_loop(0, steps // SPAN, chunk, (zero + 1.0, zero, zero), unroll=UNROLL[0])
    seg_ref[0:SEGS, :] = prod
    seg_ref[SEGS : 2 * SEGS, :] = state
    seg_ref[2 * SEGS : 3 * SEGS, :] = start
    whole, end, begin = prod[0:1], state[0:1], start[SEGS - 1 : SEGS]
    for s in range(1, SEGS):
        whole = whole * prod[s : s + 1]
        end = prod[s : s + 1] * end + state[s : s + 1]
        back = SEGS - 1 - s
        begin = start[back : back + 1] + prod[back : back + 1] * begin
    summary = jnp.concatenate([whole, end, begin, begin], axis=0)
    for k in range(sum_ref.shape[0]):
        sum_ref[k] = summary


def backward_kernel(
    steps, shards, at_ref, buf_ref, all_ref, seg_ref, conv_ref, r_ref, i_ref, a_ref, m_ref, xpad_ref, w_ref, decay_ref,
    gc_ref, wg_ref, rows_ref,
    prev_ref, gates_ref,
):
    block = w_ref.shape[0]
    shuffle = shuffle_matrix()
    mine = at_ref[0]
    decay = decay_ref[:, pl.ds(pl.multiple_of(at_ref[1] * block, block), block)]
    rate = jax.nn.softplus(-decay)
    entering = jnp.zeros((1, block), F32)
    carry_in = jnp.zeros((1, block), F32)
    for k in range(shards):
        part = all_ref[k]
        entering = jnp.where(k < mine, part[0:1] * entering + part[1:2], entering)
        back = shards - 1 - k
        part = all_ref[back]
        carry_in = jnp.where(back > mine, part[0:1] * carry_in + part[2:3], carry_in)
    heads, tails = [entering], [carry_in]
    for s in range(SEGS - 1):
        heads.append(seg_ref[s : s + 1] * heads[-1] + seg_ref[SEGS + s : SEGS + s + 1])
        back = SEGS - 1 - s
        tails.append(seg_ref[2 * SEGS + back : 2 * SEGS + back + 1] + seg_ref[back : back + 1] * tails[-1])
    state = jnp.concatenate(heads, axis=0)
    carry = jnp.concatenate(tails[::-1], axis=0)

    def ahead(c, state):
        rows = pl.ds(pl.multiple_of(c * ROWS, ROWS), ROWS)
        a, m = a_ref[rows, :], m_ref[rows, :]
        ci = conv_ref[rows, :].astype(F32) * i_ref[rows, :]
        normed = ci * m
        before = []
        for s in range(SPAN):
            at = slice(s * SEGS, (s + 1) * SEGS)
            before.append(state)
            state = a[at] * state + normed[at]
        direct = ci * a * lax.rsqrt(jnp.maximum(m * m, QFLOOR))
        prev_ref[rows, :] = a * (jnp.concatenate(before, axis=0) - direct)
        return state

    lax.fori_loop(0, steps // SPAN, ahead, state, unroll=UNROLL[1])

    def folded(v):
        return jnp.sum(v.reshape(SPAN, SEGS, block), axis=0)

    def back(k, held):
        carry, totals = held
        c = steps // SPAN - 1 - k
        base = pl.multiple_of(c * ROWS, ROWS)
        rows = pl.ds(base, ROWS)
        d = by_step(buf_ref, shuffle, steps + pl.multiple_of(c * SPAN, SPAN))
        a = a_ref[rows, :]
        grads = [None] * SPAN
        for s in range(SPAN - 1, -1, -1):
            at = slice(s * SEGS, (s + 1) * SEGS)
            grads[s] = d[at] + carry
            carry = a[at] * grads[s]
        g = jnp.concatenate(grads, axis=0)
        r, i = r_ref[rows, :], i_ref[rows, :]
        glr = g * prev_ref[rows, :] * (8.0 * r)
        gpr = (glr * ((r - 1.0) * rate)).astype(BF16)
        gim = g * (i * m_ref[rows, :])
        gpi = (gim * (conv_ref[rows, :].astype(F32) * (1.0 - i))).astype(BF16)
        both = jnp.concatenate([gpr, gpi], axis=1)
        gates_ref[rows, :] = both
        gc = gim + dot(both, w_ref[...], ((1,), (1,)))
        gc_ref[rows, :] = gc
        new = [folded(gc * xpad_ref[pl.ds(base + (3 - k) * SEGS, ROWS), :]) for k in range(4)]
        new += [folded(gc), folded(gpr.astype(F32)), folded(gpi.astype(F32)), folded(glr)]
        return carry, tuple(t + n for t, n in zip(totals, new, strict=True))

    zero = jnp.zeros((SEGS, block), F32)
    _, totals = lax.fori_loop(0, steps // SPAN, back, (carry, (zero,) * 8), unroll=UNROLL[2])
    sums = [jnp.sum(t, axis=0, keepdims=True) for t in totals]
    sums[7] = sums[7] * jax.nn.sigmoid(-decay)
    rows_ref[...] = jnp.concatenate(sums, axis=0)
    wg = dot(conv_ref[...], gates_ref[...], ((0,), (0,)))
    for s in range(SEGS):
        for q in range(4):
            for p in range(2):
                row = p * (block // 2) + s * 16
                tile = wg[row : row + 16, q * 128 : (q + 1) * 128]
                wg_ref[s * 4 + q, p * 16 : (p + 1) * 16, :] = tile.astype(BF16)


def taps_kernel(steps, at_ref, gc_ref, head_ref, taps_ref, ig_ref, tail_ref):
    block = gc_ref.shape[1]
    shuffle = shuffle_matrix()
    taps = taps_ref[:, pl.ds(pl.multiple_of(at_ref[1] * block, block), block)]
    final = steps // SPAN - 1
    tail_ref[:ROWS, :] = gc_ref[final * ROWS :, :]
    for k in range(3):
        rows = gc_ref[k * SEGS + 1 : (k + 1) * SEGS, :]
        tail_ref[ROWS + k * SEGS : ROWS + (k + 1) * SEGS, :] = jnp.concatenate([rows, head_ref[k : k + 1, :]], axis=0)

    def put(ref, base, first):
        xgrad = taps[0:1] * ref[pl.ds(base, ROWS), :]
        for k in range(1, 4):
            xgrad = xgrad + taps[k : k + 1] * ref[pl.ds(base + k * SEGS, ROWS), :]
        tiles = dot(shuffle, xgrad.astype(BF16), ((0,), (0,))).astype(BF16)
        for s in range(SEGS):
            ig_ref[s, pl.ds(first, SPAN), :] = tiles[s * SPAN : (s + 1) * SPAN]

    def turn(c, _):
        put(gc_ref, pl.multiple_of(c * ROWS, ROWS), pl.multiple_of(c * SPAN, SPAN))
        return 0

    lax.fori_loop(0, final, turn, 0, unroll=UNROLL[3])
    put(tail_ref, 0, final * SPAN)


def unpack_kernel(steps, got_ref, tiles_ref, ig_ref, recur_ref, input_ref, rows_ref):
    block = got_ref.shape[2]
    for half in range(2):
        recur_ref[:, half * 128 : (half + 1) * 128] = tiles_ref[half, :16, :]
        input_ref[:, half * 128 : (half + 1) * 128] = tiles_ref[2 + half, :16, :]
    for b in range(SEGS):
        ig_ref[0, :, b * block : (b + 1) * block] = got_ref[b, :steps, :]
        pair = got_ref[b, steps : steps + 2 * SEGS, :].astype(F32)
        row = pair[:SEGS] + pair[SEGS:]
        for k in range(SEGS):
            rows_ref[b : b + 1, k * block : (k + 1) * block] = row[k : k + 1]


def split(v):
    high = lax.reduce_precision(v, 8, 7)
    return high.astype(BF16), (v - high).astype(BF16)


def joined(high, low):
    return high.astype(F32) + low.astype(F32)


def per_device(
    shards, docs, block_input, state_cotangent, recur_weight, input_weight, gate_bias, conv_taps, conv_bias, decay_param
):
    steps, width = block_input.shape[1:]
    block = recur_weight.shape[1]
    share = recur_weight.shape[0]
    z, j = lax.axis_index("z"), lax.axis_index("j")
    at = jnp.stack([z, j]).astype(jnp.int32)
    params = (gate_bias, conv_taps, conv_bias[None], decay_param[None])

    weights = jnp.concatenate([recur_weight, input_weight], axis=0)
    weights = jnp.broadcast_to(weights[None], (shards, 2 * share, block))
    weights = lax.all_to_all(weights, "z", 0, 0).reshape(SEGS, 4 * share, block)
    halo = lax.ppermute(block_input[0, steps - 3 :], "z", [(k, k + 1) for k in range(shards - 1)])
    halo = jnp.pad(halo, ((0, 13), (0, 0)))
    tokens = (block_input[0], state_cotangent[0], halo)
    xs, ds, halo = (v.reshape(-1, SEGS, block).transpose(1, 0, 2) for v in tokens)
    at, weights = lax.optimization_barrier((at, weights))
    buf = lax.all_to_all(jnp.concatenate([xs, ds, weights, halo], axis=1), "j", 0, 0)

    total = SEGS * steps
    smem = pl.BlockSpec(memory_space=pltpu.SMEM)
    vmem = pl.BlockSpec(memory_space=pltpu.VMEM)
    shape = jax.ShapeDtypeStruct
    limit = pltpu.CompilerParams(vmem_limit_bytes=12 * 1024 * 1024)
    cost = pl.CostEstimate(flops=200 * total * block, bytes_accessed=12 * total * block, transcendentals=0)
    full, half = pltpu.VMEM((total, block), F32), pltpu.VMEM((total, block), BF16)

    def call(kernel, name, out_shape, operands, scratch=()):
        return pl.pallas_call(
            kernel,
            out_shape=out_shape,
            in_specs=[smem] + [vmem] * (len(operands) - 1),
            out_specs=(vmem,) * len(out_shape),
            scratch_shapes=scratch,
            compiler_params=limit,
            cost_estimate=cost,
            name=name,
        )(*operands)

    conv, r, i, a, m, xpad, seg, summary, w = call(
        functools.partial(forward_kernel, steps),
        "forward",
        (half, full, full, full, full, pltpu.VMEM((total + 3 * SEGS, block), F32), shape((3 * SEGS, block), F32))
        + (shape((shards, 4, block), F32), shape((block, 2 * block), BF16)),
        (at, buf, *params),
    )
    everyone = lax.all_to_all(summary, "z", 0, 0)
    gc, wg, rows = call(
        functools.partial(backward_kernel, steps, shards),
        "backward",
        (full, shape((4 * SEGS, 32, 128), BF16), shape((8, block), F32)),
        (at, buf, everyone, seg, conv, r, i, a, m, xpad, w, params[3]),
        [pltpu.VMEM((total, block), F32), pltpu.VMEM((total, 2 * block), BF16)],
    )
    head = gc[: 3 * SEGS].reshape(3, SEGS, block)[:, 0]
    head = lax.ppermute(head, "z", [(k + 1, k) for k in range(shards - 1)])
    quarter = block // docs
    packed = jnp.concatenate(split(rows.reshape(SEGS * docs, 1, quarter)), axis=2)
    got = lax.all_to_all(jnp.concatenate([wg, packed], axis=1), ("j", "doc"), 0, 0)
    got = got.reshape(SEGS, docs, 33, 128)
    wsum = jnp.sum(got[:, :, :32].astype(F32), axis=1).reshape(shards, 16, 128)
    csum = jnp.sum(joined(got[:, :, 32, :quarter], got[:, :, 32, quarter:]), axis=1)
    csum = jnp.broadcast_to(csum.reshape(1, 4, 128), (shards, 4, 128))
    got = lax.all_to_all(jnp.concatenate((wsum.astype(BF16),) + split(csum), axis=1), "z", 0, 0)
    (ig,) = call(
        functools.partial(taps_kernel, steps),
        "taps",
        (shape((SEGS, steps, block), BF16),),
        (at, gc, head, conv_taps),
        [pltpu.VMEM((ROWS + 3 * SEGS, block), F32)],
    )
    wsum = jnp.sum(got[:, :16].astype(F32), axis=0)
    csum = jnp.sum(joined(got[:, 16:20], got[:, 20:]), axis=0)
    send, ig = lax.optimization_barrier((jnp.concatenate([wsum, csum], axis=0), ig))
    tiles = lax.all_to_all(jnp.broadcast_to(send[None], (docs, 20, 128)), "doc", 0, 0)
    csum = tiles[:, 16:].reshape(docs, SEGS, quarter).transpose(1, 0, 2).reshape(SEGS, block)
    csum = jnp.broadcast_to(jnp.concatenate(split(csum), axis=0)[None], (SEGS, 2 * SEGS, block))
    got = lax.all_to_all(jnp.concatenate([ig, csum], axis=1), "j", 0, 0)
    return pl.pallas_call(
        functools.partial(unpack_kernel, steps),
        out_shape=(
            shape((1, steps, width), BF16), shape((share, block), F32), shape((share, block), F32), shape((SEGS, width), F32)
        ),
        in_specs=[vmem] * 2,
        out_specs=(vmem,) * 4,
        compiler_params=limit,
        name="unpack",
    )(got, tiles)


def solution(mesh):
    seq, docs = mesh.shape["seq"], mesh.shape["doc"]
    shards = seq // SEGS
    fine = Mesh(mesh.devices.reshape(shards, SEGS, docs), ("z", "j", "doc"))
    tokens, rows = P("doc", ("z", "j"), None), P(("z", "j"), None)
    return jax.shard_map(
        functools.partial(per_device, shards, docs),
        mesh=fine,
        in_specs=(tokens, tokens, rows, rows, P(), P(), P(), P()),
        out_specs=(tokens, rows, rows, P()),
        check_vma=False,
    )
```

```python
import functools

import jax
import jax.numpy as jnp
from jax import lax
from jax.experimental import pallas as pl
from jax.experimental.pallas import tpu as pltpu
from jax.sharding import Mesh
from jax.sharding import PartitionSpec as P

QFLOOR = 0.001
SEGS = 8
SPAN = 16
ROWS = SEGS * SPAN
UNROLL = (True, True, True, True)
F32 = jnp.float32
BF16 = jnp.bfloat16


def dot(a, b, contract=((1,), (0,))):
    return lax.dot_general(a, b, (contract, ((), ())), preferred_element_type=F32)


def shuffle_matrix():
    row = lax.broadcasted_iota(jnp.int32, (ROWS, ROWS), 0)
    col = lax.broadcasted_iota(jnp.int32, (ROWS, ROWS), 1)
    return jnp.where(col == (row % SEGS) * SPAN + row // SEGS, 1.0, 0.0).astype(BF16)


def by_step(buf_ref, shuffle, first):
    tiles = [buf_ref[s, pl.ds(first, SPAN), :] for s in range(SEGS)]
    return dot(shuffle, jnp.concatenate(tiles, axis=0))


def load_weights(buf_ref, w_ref, first):
    block = w_ref.shape[0]
    for s in range(SEGS):
        for p in range(2):
            for w in range(2):
                row, at = p * (block // 2) + s * 16, first + (p * 2 + w) * 16
                w_ref[row : row + 16, w * block : (w + 1) * block] = buf_ref[s, at : at + 16, :]


def one_minus_square(a, decay):
    x = 2.0 * decay
    series = x * (1.0 - x * (1 / 2) * (1.0 - x * (1 / 3)))
    return jnp.where(x < 0.0078125, series, 1.0 - a * a)


def sigmoid(x):
    return pl.reciprocal(1.0 + jnp.exp(-x), approx=True)


def block_params(at_ref, bias_ref, taps_ref, cbias_ref, decay_ref, block):
    lanes = pl.ds(pl.multiple_of(at_ref[1] * block, block), block)
    rate = jax.nn.softplus(-decay_ref[:, lanes])
    return bias_ref[:, lanes], taps_ref[:, lanes], cbias_ref[:, lanes], rate


def forward_kernel(
    steps, at_ref, buf_ref, halo_ref, bias_ref, taps_ref, cbias_ref, decay_ref,
    conv_ref, r_ref, i_ref, a_ref, m_ref, xpad_ref, seg_ref, sum_ref, w_ref,
):
    block = w_ref.shape[0]
    shuffle = shuffle_matrix()
    load_weights(buf_ref, w_ref, 2 * steps)
    bias, taps, cbias, rate = block_params(at_ref, bias_ref, taps_ref, cbias_ref, decay_ref, block)
    rate8 = 8.0 * rate
    last = by_step(buf_ref, shuffle, steps - SPAN)[ROWS - 3 * SEGS :]
    halo = jnp.where(at_ref[0] > 0, halo_ref[...], 0.0)
    for k in range(3):
        rows = last[k * SEGS : (k + 1) * SEGS]
        xpad_ref[k * SEGS : (k + 1) * SEGS, :] = jnp.concatenate(
            [halo[k : k + 1], rows[: SEGS - 1]], axis=0
        )

    def chunk(c, carry):
        prod, state, start = carry
        base = pl.multiple_of(c * ROWS, ROWS)
        first = pl.multiple_of(c * SPAN, SPAN)
        x = by_step(buf_ref, shuffle, first)
        d = by_step(buf_ref, shuffle, steps + first)
        xpad_ref[pl.ds(base + 3 * SEGS, ROWS), :] = x
        conv = cbias + taps[0:1] * x
        for k in range(1, 4):
            conv = conv + taps[k : k + 1] * xpad_ref[pl.ds(base + (3 - k) * SEGS, ROWS), :]
        conv_b = conv.astype(BF16)
        conv_ref[pl.ds(base, ROWS), :] = conv_b
        conv_v = conv_b.astype(F32)
        pre = dot(conv_b, w_ref[...])
        r = sigmoid(pre[:, :block] + bias[0:1])
        i = sigmoid(pre[:, block:] + bias[1:2])
        decay = r * rate8
        a = jnp.exp(-decay)
        q = one_minus_square(a, decay)
        m = q * lax.rsqrt(jnp.maximum(q, 1e-37))
        r_ref[pl.ds(base, ROWS), :] = r
        i_ref[pl.ds(base, ROWS), :] = i
        a_ref[pl.ds(base, ROWS), :] = a
        m_ref[pl.ds(base, ROWS), :] = m
        normed = conv_v * i * m
        for s in range(SPAN):
            rows = slice(s * SEGS, (s + 1) * SEGS)
            prod = prod * a[rows]
            state = a[rows] * state + normed[rows]
            start = start + prod * d[rows]
        return prod, state, start

    zero = jnp.zeros((SEGS, block), F32)
    prod, state, start = lax.fori_loop(0, steps // SPAN, chunk, (zero + 1.0, zero, zero), unroll=UNROLL[0])
    seg_ref[0:SEGS, :] = prod
    seg_ref[SEGS : 2 * SEGS, :] = state
    seg_ref[2 * SEGS : 3 * SEGS, :] = start
    whole, end, begin = prod[0:1], state[0:1], start[SEGS - 1 : SEGS]
    for s in range(1, SEGS):
        whole = whole * prod[s : s + 1]
        end = prod[s : s + 1] * end + state[s : s + 1]
        back = SEGS - 1 - s
        begin = start[back : back + 1] + prod[back : back + 1] * begin
    summary = jnp.concatenate([whole, end, begin], axis=1)
    for k in range(sum_ref.shape[0]):
        sum_ref[k] = summary


def backward_kernel(
    steps, shards, at_ref, buf_ref, all_ref, seg_ref, conv_ref, r_ref, i_ref, a_ref, m_ref, xpad_ref, w_ref, decay_ref,
    gc_ref, wg_ref, rows_ref,
    prev_ref, gates_ref,
):
    block = w_ref.shape[0]
    shuffle = shuffle_matrix()
    mine = at_ref[0]
    decay = decay_ref[:, pl.ds(pl.multiple_of(at_ref[1] * block, block), block)]
    rate = jax.nn.softplus(-decay)
    entering = jnp.zeros((1, block), F32)
    carry_in = jnp.zeros((1, block), F32)
    for k in range(shards):
        part = all_ref[k]
        entering = jnp.where(k < mine, part[:, :block] * entering + part[:, block : 2 * block], entering)
        back = shards - 1 - k
        part = all_ref[back]
        carry_in = jnp.where(back > mine, part[:, :block] * carry_in + part[:, 2 * block :], carry_in)
    heads, tails = [entering], [carry_in]
    for s in range(SEGS - 1):
        heads.append(seg_ref[s : s + 1] * heads[-1] + seg_ref[SEGS + s : SEGS + s + 1])
        back = SEGS - 1 - s
        tails.append(seg_ref[2 * SEGS + back : 2 * SEGS + back + 1] + seg_ref[back : back + 1] * tails[-1])
    state = jnp.concatenate(heads, axis=0)
    carry = jnp.concatenate(tails[::-1], axis=0)

    def ahead(c, state):
        rows = pl.ds(pl.multiple_of(c * ROWS, ROWS), ROWS)
        a, m = a_ref[rows, :], m_ref[rows, :]
        ci = conv_ref[rows, :].astype(F32) * i_ref[rows, :]
        normed = ci * m
        before = []
        for s in range(SPAN):
            at = slice(s * SEGS, (s + 1) * SEGS)
            before.append(state)
            state = a[at] * state + normed[at]
        direct = ci * a * lax.rsqrt(jnp.maximum(m * m, QFLOOR))
        prev_ref[rows, :] = a * (jnp.concatenate(before, axis=0) - direct)
        return state

    lax.fori_loop(0, steps // SPAN, ahead, state, unroll=UNROLL[1])

    def folded(v):
        return jnp.sum(v.reshape(SPAN, SEGS, block), axis=0)

    def back(k, held):
        carry, totals = held
        c = steps // SPAN - 1 - k
        base = pl.multiple_of(c * ROWS, ROWS)
        rows = pl.ds(base, ROWS)
        d = by_step(buf_ref, shuffle, steps + pl.multiple_of(c * SPAN, SPAN))
        a = a_ref[rows, :]
        grads = [None] * SPAN
        for s in range(SPAN - 1, -1, -1):
            at = slice(s * SEGS, (s + 1) * SEGS)
            grads[s] = d[at] + carry
            carry = a[at] * grads[s]
        g = jnp.concatenate(grads, axis=0)
        r, i = r_ref[rows, :], i_ref[rows, :]
        glr = g * prev_ref[rows, :] * (8.0 * r)
        gpr = (glr * ((r - 1.0) * rate)).astype(BF16)
        gim = g * (i * m_ref[rows, :])
        gpi = (gim * (conv_ref[rows, :].astype(F32) * (1.0 - i))).astype(BF16)
        both = jnp.concatenate([gpr, gpi], axis=1)
        gates_ref[rows, :] = both
        gc = gim + dot(both, w_ref[...], ((1,), (1,)))
        gc_ref[rows, :] = gc
        new = [folded(gc * xpad_ref[pl.ds(base + (3 - k) * SEGS, ROWS), :]) for k in range(4)]
        new += [folded(gc), folded(gpr.astype(F32)), folded(gpi.astype(F32)), folded(glr)]
        return carry, tuple(t + n for t, n in zip(totals, new, strict=True))

    zero = jnp.zeros((SEGS, block), F32)
    _, totals = lax.fori_loop(0, steps // SPAN, back, (carry, (zero,) * 8), unroll=UNROLL[2])
    sums = [jnp.sum(t, axis=0, keepdims=True) for t in totals]
    sums[7] = sums[7] * jax.nn.sigmoid(-decay)
    rows_ref[...] = jnp.concatenate(sums, axis=0)
    wg = dot(conv_ref[...], gates_ref[...], ((0,), (0,)))
    for s in range(SEGS):
        for q in range(4):
            for p in range(2):
                row = p * (block // 2) + s * 16
                tile = wg[row : row + 16, q * 128 : (q + 1) * 128]
                wg_ref[s * 4 + q, p * 16 : (p + 1) * 16, :] = tile.astype(BF16)


def taps_kernel(steps, at_ref, gc_ref, head_ref, taps_ref, ig_ref, tail_ref):
    block = gc_ref.shape[1]
    shuffle = shuffle_matrix()
    taps = taps_ref[:, pl.ds(pl.multiple_of(at_ref[1] * block, block), block)]
    final = steps // SPAN - 1
    tail_ref[:ROWS, :] = gc_ref[final * ROWS :, :]
    for k in range(3):
        rows = gc_ref[k * SEGS + 1 : (k + 1) * SEGS, :]
        tail_ref[ROWS + k * SEGS : ROWS + (k + 1) * SEGS, :] = jnp.concatenate([rows, head_ref[k : k + 1, :]], axis=0)

    def put(ref, base, first):
        xgrad = taps[0:1] * ref[pl.ds(base, ROWS), :]
        for k in range(1, 4):
            xgrad = xgrad + taps[k : k + 1] * ref[pl.ds(base + k * SEGS, ROWS), :]
        tiles = dot(shuffle, xgrad.astype(BF16), ((0,), (0,))).astype(BF16)
        for s in range(SEGS):
            ig_ref[s, pl.ds(first, SPAN), :] = tiles[s * SPAN : (s + 1) * SPAN]

    def turn(c, _):
        put(gc_ref, pl.multiple_of(c * ROWS, ROWS), pl.multiple_of(c * SPAN, SPAN))
        return 0

    lax.fori_loop(0, final, turn, 0, unroll=UNROLL[3])
    put(tail_ref, 0, final * SPAN)


def unpack_kernel(steps, got_ref, tiles_ref, ig_ref, recur_ref, input_ref, rows_ref):
    block = got_ref.shape[2]
    for half in range(2):
        recur_ref[:, half * 128 : (half + 1) * 128] = tiles_ref[half, :16, :]
        input_ref[:, half * 128 : (half + 1) * 128] = tiles_ref[2 + half, :16, :]
    for b in range(SEGS):
        ig_ref[0, :, b * block : (b + 1) * block] = got_ref[b, :steps, :]
        pair = got_ref[b, steps : steps + 2 * SEGS, :].astype(F32)
        row = pair[:SEGS] + pair[SEGS:]
        for k in range(SEGS):
            rows_ref[b : b + 1, k * block : (k + 1) * block] = row[k : k + 1]


def split(v):
    high = lax.reduce_precision(v, 8, 7)
    return high.astype(BF16), (v - high).astype(BF16)


def joined(high, low):
    return high.astype(F32) + low.astype(F32)


def per_device(
    shards, docs, block_input, state_cotangent, recur_weight, input_weight, gate_bias, conv_taps, conv_bias, decay_param
):
    steps, width = block_input.shape[1:]
    block = recur_weight.shape[1]
    share = recur_weight.shape[0]
    z, j = lax.axis_index("z"), lax.axis_index("j")
    at = jnp.stack([z, j]).astype(jnp.int32)
    params = (gate_bias, conv_taps, conv_bias[None], decay_param[None])

    weights = jnp.concatenate([recur_weight, input_weight], axis=0)
    weights = jnp.broadcast_to(weights[None], (shards, 2 * share, block))
    weights = lax.all_to_all(weights, "z", 0, 0).reshape(SEGS, 4 * share, block)
    halo = lax.ppermute(block_input[0, steps - 3 :], "z", [(k, k + 1) for k in range(shards - 1)])
    halo = jnp.pad(halo, ((0, 5), (0, 0)))
    tokens = (block_input[0], state_cotangent[0], halo)
    xs, ds, halo = (v.reshape(-1, SEGS, block).transpose(1, 0, 2) for v in tokens)
    at, weights = lax.optimization_barrier((at, weights))
    buf = lax.all_to_all(jnp.concatenate([xs, ds, weights, halo], axis=1), "j", 0, 0)
    halo = buf[SEGS - 1, 2 * steps + 4 * share :].astype(F32)

    total = SEGS * steps
    smem = pl.BlockSpec(memory_space=pltpu.SMEM)
    vmem = pl.BlockSpec(memory_space=pltpu.VMEM)
    shape = jax.ShapeDtypeStruct
    limit = pltpu.CompilerParams(vmem_limit_bytes=12 * 1024 * 1024)
    cost = pl.CostEstimate(flops=200 * total * block, bytes_accessed=12 * total * block, transcendentals=0)
    full, half = pltpu.VMEM((total, block), F32), pltpu.VMEM((total, block), BF16)

    def call(kernel, name, out_shape, operands, scratch=()):
        return pl.pallas_call(
            kernel,
            out_shape=out_shape,
            in_specs=[smem] + [vmem] * (len(operands) - 1),
            out_specs=(vmem,) * len(out_shape),
            scratch_shapes=scratch,
            compiler_params=limit,
            cost_estimate=cost,
            name=name,
        )(*operands)

    conv, r, i, a, m, xpad, seg, summary, w = call(
        functools.partial(forward_kernel, steps),
        "forward",
        (half, full, full, full, full, pltpu.VMEM((total + 3 * SEGS, block), F32), shape((3 * SEGS, block), F32))
        + (shape((shards, 1, 3 * block), F32), shape((block, 2 * block), BF16)),
        (at, buf, halo, *params),
    )
    everyone = lax.all_to_all(summary, "z", 0, 0)
    gc, wg, rows = call(
        functools.partial(backward_kernel, steps, shards),
        "backward",
        (full, shape((4 * SEGS, 32, 128), BF16), shape((8, block), F32)),
        (at, buf, everyone, seg, conv, r, i, a, m, xpad, w, params[3]),
        [pltpu.VMEM((total, block), F32), pltpu.VMEM((total, 2 * block), BF16)],
    )
    head = gc[: 3 * SEGS].reshape(3, SEGS, block)[:, 0]
    head = lax.ppermute(head, "z", [(k + 1, k) for k in range(shards - 1)])
    quarter = block // docs
    packed = jnp.concatenate(split(rows.reshape(SEGS * docs, 1, quarter)), axis=2)
    got = lax.all_to_all(jnp.concatenate([wg, packed], axis=1), ("j", "doc"), 0, 0)
    got = got.reshape(SEGS, docs, 33, 128)
    wsum = jnp.sum(got[:, :, :32].astype(F32), axis=1).reshape(shards, 16, 128)
    csum = jnp.sum(joined(got[:, :, 32, :quarter], got[:, :, 32, quarter:]), axis=1)
    csum = jnp.broadcast_to(csum.reshape(1, 4, 128), (shards, 4, 128))
    got = lax.all_to_all(jnp.concatenate((wsum.astype(BF16),) + split(csum), axis=1), "z", 0, 0)
    (ig,) = call(
        functools.partial(taps_kernel, steps),
        "taps",
        (shape((SEGS, steps, block), BF16),),
        (at, gc, head, conv_taps),
        [pltpu.VMEM((ROWS + 3 * SEGS, block), F32)],
    )
    wsum = jnp.sum(got[:, :16].astype(F32), axis=0)
    csum = jnp.sum(joined(got[:, 16:20], got[:, 20:]), axis=0)
    send, ig = lax.optimization_barrier((jnp.concatenate([wsum, csum], axis=0), ig))
    tiles = lax.all_to_all(jnp.broadcast_to(send[None], (docs, 20, 128)), "doc", 0, 0)
    csum = tiles[:, 16:].reshape(docs, SEGS, quarter).transpose(1, 0, 2).reshape(SEGS, block)
    csum = jnp.broadcast_to(jnp.concatenate(split(csum), axis=0)[None], (SEGS, 2 * SEGS, block))
    got = lax.all_to_all(jnp.concatenate([ig, csum], axis=1), "j", 0, 0)
    return pl.pallas_call(
        functools.partial(unpack_kernel, steps),
        out_shape=(
            shape((1, steps, width), BF16), shape((share, block), F32), shape((share, block), F32), shape((SEGS, width), F32)
        ),
        in_specs=[vmem] * 2,
        out_specs=(vmem,) * 4,
        compiler_params=limit,
        name="unpack",
    )(got, tiles)


def solution(mesh):
    seq, docs = mesh.shape["seq"], mesh.shape["doc"]
    shards = seq // SEGS
    fine = Mesh(mesh.devices.reshape(shards, SEGS, docs), ("z", "j", "doc"))
    tokens, rows = P("doc", ("z", "j"), None), P(("z", "j"), None)
    return jax.shard_map(
        functools.partial(per_device, shards, docs),
        mesh=fine,
        in_specs=(tokens, tokens, rows, rows, P(), P(), P(), P()),
        out_specs=(tokens, rows, rows, P()),
        check_vma=False,
    )
```

```python
import functools

import jax
import jax.numpy as jnp
from jax import lax
from jax.experimental import pallas as pl
from jax.experimental.pallas import tpu as pltpu
from jax.sharding import Mesh
from jax.sharding import PartitionSpec as P

QFLOOR = 0.001
SEGS = 8
SPAN = 32
ROWS = SEGS * SPAN
UNROLL = (True, True, True, True)
F32 = jnp.float32
BF16 = jnp.bfloat16


def dot(a, b, contract=((1,), (0,))):
    return lax.dot_general(a, b, (contract, ((), ())), preferred_element_type=F32)


def shuffle_matrix():
    row = lax.broadcasted_iota(jnp.int32, (ROWS, ROWS), 0)
    col = lax.broadcasted_iota(jnp.int32, (ROWS, ROWS), 1)
    return jnp.where(col == (row % SEGS) * SPAN + row // SEGS, 1.0, 0.0).astype(BF16)


def by_step(buf_ref, shuffle, first):
    tiles = [buf_ref[s, pl.ds(first, SPAN), :] for s in range(SEGS)]
    return dot(shuffle, jnp.concatenate(tiles, axis=0))


def load_weights(buf_ref, w_ref, first):
    block = w_ref.shape[0]
    for s in range(SEGS):
        for p in range(2):
            for w in range(2):
                row, at = p * (block // 2) + s * 16, first + (p * 2 + w) * 16
                w_ref[row : row + 16, w * block : (w + 1) * block] = buf_ref[s, at : at + 16, :]


def one_minus_square(a, decay):
    x = 2.0 * decay
    series = x * (1.0 - x * (1 / 2) * (1.0 - x * (1 / 3)))
    return jnp.where(x < 0.0078125, series, 1.0 - a * a)


def sigmoid(x):
    return pl.reciprocal(1.0 + jnp.exp(-x), approx=True)


def block_params(at_ref, bias_ref, taps_ref, cbias_ref, decay_ref, block):
    lanes = pl.ds(pl.multiple_of(at_ref[1] * block, block), block)
    rate = jax.nn.softplus(-decay_ref[:, lanes])
    return bias_ref[:, lanes], taps_ref[:, lanes], cbias_ref[:, lanes], rate


def forward_kernel(
    steps, at_ref, buf_ref, halo_ref, bias_ref, taps_ref, cbias_ref, decay_ref,
    conv_ref, r_ref, i_ref, a_ref, m_ref, xpad_ref, seg_ref, sum_ref, w_ref,
):
    block = w_ref.shape[0]
    shuffle = shuffle_matrix()
    load_weights(buf_ref, w_ref, 2 * steps)
    bias, taps, cbias, rate = block_params(at_ref, bias_ref, taps_ref, cbias_ref, decay_ref, block)
    rate8 = 8.0 * rate
    last = by_step(buf_ref, shuffle, steps - SPAN)[ROWS - 3 * SEGS :]
    halo = jnp.where(at_ref[0] > 0, halo_ref[...], 0.0)
    for k in range(3):
        rows = last[k * SEGS : (k + 1) * SEGS]
        xpad_ref[k * SEGS : (k + 1) * SEGS, :] = jnp.concatenate(
            [halo[k : k + 1], rows[: SEGS - 1]], axis=0
        )

    def chunk(c, carry):
        prod, state, start = carry
        base = pl.multiple_of(c * ROWS, ROWS)
        first = pl.multiple_of(c * SPAN, SPAN)
        x = by_step(buf_ref, shuffle, first)
        d = by_step(buf_ref, shuffle, steps + first)
        xpad_ref[pl.ds(base + 3 * SEGS, ROWS), :] = x
        conv = cbias + taps[0:1] * x
        for k in range(1, 4):
            conv = conv + taps[k : k + 1] * xpad_ref[pl.ds(base + (3 - k) * SEGS, ROWS), :]
        conv_b = conv.astype(BF16)
        conv_ref[pl.ds(base, ROWS), :] = conv_b
        conv_v = conv_b.astype(F32)
        pre = dot(conv_b, w_ref[...])
        r = sigmoid(pre[:, :block] + bias[0:1])
        i = sigmoid(pre[:, block:] + bias[1:2])
        decay = r * rate8
        a = jnp.exp(-decay)
        q = one_minus_square(a, decay)
        m = q * lax.rsqrt(jnp.maximum(q, 1e-37))
        r_ref[pl.ds(base, ROWS), :] = r
        i_ref[pl.ds(base, ROWS), :] = i
        a_ref[pl.ds(base, ROWS), :] = a
        m_ref[pl.ds(base, ROWS), :] = m
        normed = conv_v * i * m
        for s in range(SPAN):
            rows = slice(s * SEGS, (s + 1) * SEGS)
            prod = prod * a[rows]
            state = a[rows] * state + normed[rows]
            start = start + prod * d[rows]
        return prod, state, start

    zero = jnp.zeros((SEGS, block), F32)
    prod, state, start = lax.fori_loop(0, steps // SPAN, chunk, (zero + 1.0, zero, zero), unroll=UNROLL[0])
    seg_ref[0:SEGS, :] = prod
    seg_ref[SEGS : 2 * SEGS, :] = state
    seg_ref[2 * SEGS : 3 * SEGS, :] = start
    whole, end, begin = prod[0:1], state[0:1], start[SEGS - 1 : SEGS]
    for s in range(1, SEGS):
        whole = whole * prod[s : s + 1]
        end = prod[s : s + 1] * end + state[s : s + 1]
        back = SEGS - 1 - s
        begin = start[back : back + 1] + prod[back : back + 1] * begin
    summary = jnp.concatenate([whole, end, begin], axis=1)
    for k in range(sum_ref.shape[0]):
        sum_ref[k] = summary


def backward_kernel(
    steps, shards, at_ref, buf_ref, all_ref, seg_ref, conv_ref, r_ref, i_ref, a_ref, m_ref, xpad_ref, w_ref, decay_ref,
    gc_ref, wg_ref, rows_ref,
    prev_ref, gates_ref,
):
    block = w_ref.shape[0]
    shuffle = shuffle_matrix()
    mine = at_ref[0]
    decay = decay_ref[:, pl.ds(pl.multiple_of(at_ref[1] * block, block), block)]
    rate = jax.nn.softplus(-decay)
    entering = jnp.zeros((1, block), F32)
    carry_in = jnp.zeros((1, block), F32)
    for k in range(shards):
        part = all_ref[k]
        entering = jnp.where(k < mine, part[:, :block] * entering + part[:, block : 2 * block], entering)
        back = shards - 1 - k
        part = all_ref[back]
        carry_in = jnp.where(back > mine, part[:, :block] * carry_in + part[:, 2 * block :], carry_in)
    heads, tails = [entering], [carry_in]
    for s in range(SEGS - 1):
        heads.append(seg_ref[s : s + 1] * heads[-1] + seg_ref[SEGS + s : SEGS + s + 1])
        back = SEGS - 1 - s
        tails.append(seg_ref[2 * SEGS + back : 2 * SEGS + back + 1] + seg_ref[back : back + 1] * tails[-1])
    state = jnp.concatenate(heads, axis=0)
    carry = jnp.concatenate(tails[::-1], axis=0)

    def ahead(c, state):
        rows = pl.ds(pl.multiple_of(c * ROWS, ROWS), ROWS)
        a, m = a_ref[rows, :], m_ref[rows, :]
        ci = conv_ref[rows, :].astype(F32) * i_ref[rows, :]
        normed = ci * m
        before = []
        for s in range(SPAN):
            at = slice(s * SEGS, (s + 1) * SEGS)
            before.append(state)
            state = a[at] * state + normed[at]
        direct = ci * a * lax.rsqrt(jnp.maximum(m * m, QFLOOR))
        prev_ref[rows, :] = a * (jnp.concatenate(before, axis=0) - direct)
        return state

    lax.fori_loop(0, steps // SPAN, ahead, state, unroll=UNROLL[1])

    def folded(v):
        return jnp.sum(v.reshape(SPAN, SEGS, block), axis=0)

    def back(k, held):
        carry, totals = held
        c = steps // SPAN - 1 - k
        base = pl.multiple_of(c * ROWS, ROWS)
        rows = pl.ds(base, ROWS)
        d = by_step(buf_ref, shuffle, steps + pl.multiple_of(c * SPAN, SPAN))
        a = a_ref[rows, :]
        grads = [None] * SPAN
        for s in range(SPAN - 1, -1, -1):
            at = slice(s * SEGS, (s + 1) * SEGS)
            grads[s] = d[at] + carry
            carry = a[at] * grads[s]
        g = jnp.concatenate(grads, axis=0)
        r, i = r_ref[rows, :], i_ref[rows, :]
        glr = g * prev_ref[rows, :] * (8.0 * r)
        gpr = (glr * ((r - 1.0) * rate)).astype(BF16)
        gim = g * (i * m_ref[rows, :])
        gpi = (gim * (conv_ref[rows, :].astype(F32) * (1.0 - i))).astype(BF16)
        both = jnp.concatenate([gpr, gpi], axis=1)
        gates_ref[rows, :] = both
        gc = gim + dot(both, w_ref[...], ((1,), (1,)))
        gc_ref[rows, :] = gc
        new = [folded(gc * xpad_ref[pl.ds(base + (3 - k) * SEGS, ROWS), :]) for k in range(4)]
        new += [folded(gc), folded(gpr.astype(F32)), folded(gpi.astype(F32)), folded(glr)]
        return carry, tuple(t + n for t, n in zip(totals, new, strict=True))

    zero = jnp.zeros((SEGS, block), F32)
    _, totals = lax.fori_loop(0, steps // SPAN, back, (carry, (zero,) * 8), unroll=UNROLL[2])
    sums = [jnp.sum(t, axis=0, keepdims=True) for t in totals]
    sums[7] = sums[7] * jax.nn.sigmoid(-decay)
    rows_ref[...] = jnp.concatenate(sums, axis=0)
    wg = dot(conv_ref[...], gates_ref[...], ((0,), (0,)))
    for s in range(SEGS):
        for q in range(4):
            for p in range(2):
                row = p * (block // 2) + s * 16
                tile = wg[row : row + 16, q * 128 : (q + 1) * 128]
                wg_ref[s * 4 + q, p * 16 : (p + 1) * 16, :] = tile.astype(BF16)


def taps_kernel(steps, at_ref, gc_ref, head_ref, taps_ref, ig_ref, tail_ref):
    block = gc_ref.shape[1]
    shuffle = shuffle_matrix()
    taps = taps_ref[:, pl.ds(pl.multiple_of(at_ref[1] * block, block), block)]
    final = steps // SPAN - 1
    tail_ref[:ROWS, :] = gc_ref[final * ROWS :, :]
    for k in range(3):
        rows = gc_ref[k * SEGS + 1 : (k + 1) * SEGS, :]
        tail_ref[ROWS + k * SEGS : ROWS + (k + 1) * SEGS, :] = jnp.concatenate([rows, head_ref[k : k + 1, :]], axis=0)

    def put(ref, base, first):
        xgrad = taps[0:1] * ref[pl.ds(base, ROWS), :]
        for k in range(1, 4):
            xgrad = xgrad + taps[k : k + 1] * ref[pl.ds(base + k * SEGS, ROWS), :]
        tiles = dot(shuffle, xgrad.astype(BF16), ((0,), (0,))).astype(BF16)
        for s in range(SEGS):
            ig_ref[s, pl.ds(first, SPAN), :] = tiles[s * SPAN : (s + 1) * SPAN]

    def turn(c, _):
        put(gc_ref, pl.multiple_of(c * ROWS, ROWS), pl.multiple_of(c * SPAN, SPAN))
        return 0

    lax.fori_loop(0, final, turn, 0, unroll=UNROLL[3])
    put(tail_ref, 0, final * SPAN)


def unpack_kernel(steps, got_ref, tiles_ref, ig_ref, recur_ref, input_ref, rows_ref):
    block = got_ref.shape[2]
    for half in range(2):
        recur_ref[:, half * 128 : (half + 1) * 128] = tiles_ref[half, :16, :]
        input_ref[:, half * 128 : (half + 1) * 128] = tiles_ref[2 + half, :16, :]
    for b in range(SEGS):
        ig_ref[0, :, b * block : (b + 1) * block] = got_ref[b, :steps, :]
        pair = got_ref[b, steps : steps + 2 * SEGS, :].astype(F32)
        row = pair[:SEGS] + pair[SEGS:]
        for k in range(SEGS):
            rows_ref[b : b + 1, k * block : (k + 1) * block] = row[k : k + 1]


def split(v):
    high = lax.reduce_precision(v, 8, 7)
    return high.astype(BF16), (v - high).astype(BF16)


def joined(high, low):
    return high.astype(F32) + low.astype(F32)


def per_device(
    shards, docs, block_input, state_cotangent, recur_weight, input_weight, gate_bias, conv_taps, conv_bias, decay_param
):
    steps, width = block_input.shape[1:]
    block = recur_weight.shape[1]
    share = recur_weight.shape[0]
    z, j = lax.axis_index("z"), lax.axis_index("j")
    at = jnp.stack([z, j]).astype(jnp.int32)
    params = (gate_bias, conv_taps, conv_bias[None], decay_param[None])

    weights = jnp.concatenate([recur_weight, input_weight], axis=0)
    weights = jnp.broadcast_to(weights[None], (shards, 2 * share, block))
    weights = lax.all_to_all(weights, "z", 0, 0).reshape(SEGS, 4 * share, block)
    halo = lax.ppermute(block_input[0, steps - 3 :], "z", [(k, k + 1) for k in range(shards - 1)])
    halo = jnp.pad(halo, ((0, 5), (0, 0)))
    tokens = (block_input[0], state_cotangent[0], halo)
    xs, ds, halo = (v.reshape(-1, SEGS, block).transpose(1, 0, 2) for v in tokens)
    at, weights = lax.optimization_barrier((at, weights))
    buf = lax.all_to_all(jnp.concatenate([xs, ds, weights, halo], axis=1), "j", 0, 0)
    halo = buf[SEGS - 1, 2 * steps + 4 * share :].astype(F32)

    total = SEGS * steps
    smem = pl.BlockSpec(memory_space=pltpu.SMEM)
    vmem = pl.BlockSpec(memory_space=pltpu.VMEM)
    shape = jax.ShapeDtypeStruct
    limit = pltpu.CompilerParams(vmem_limit_bytes=12 * 1024 * 1024)
    cost = pl.CostEstimate(flops=200 * total * block, bytes_accessed=12 * total * block, transcendentals=0)
    full, half = pltpu.VMEM((total, block), F32), pltpu.VMEM((total, block), BF16)

    def call(kernel, name, out_shape, operands, scratch=()):
        return pl.pallas_call(
            kernel,
            out_shape=out_shape,
            in_specs=[smem] + [vmem] * (len(operands) - 1),
            out_specs=(vmem,) * len(out_shape),
            scratch_shapes=scratch,
            compiler_params=limit,
            cost_estimate=cost,
            name=name,
        )(*operands)

    conv, r, i, a, m, xpad, seg, summary, w = call(
        functools.partial(forward_kernel, steps),
        "forward",
        (half, full, full, full, full, pltpu.VMEM((total + 3 * SEGS, block), F32), shape((3 * SEGS, block), F32))
        + (shape((shards, 1, 3 * block), F32), shape((block, 2 * block), BF16)),
        (at, buf, halo, *params),
    )
    everyone = lax.all_to_all(summary, "z", 0, 0)
    gc, wg, rows = call(
        functools.partial(backward_kernel, steps, shards),
        "backward",
        (full, shape((4 * SEGS, 32, 128), BF16), shape((8, block), F32)),
        (at, buf, everyone, seg, conv, r, i, a, m, xpad, w, params[3]),
        [pltpu.VMEM((total, block), F32), pltpu.VMEM((total, 2 * block), BF16)],
    )
    head = gc[: 3 * SEGS].reshape(3, SEGS, block)[:, 0]
    head = lax.ppermute(head, "z", [(k + 1, k) for k in range(shards - 1)])
    quarter = block // docs
    packed = jnp.concatenate(split(rows.reshape(SEGS * docs, 1, quarter)), axis=2)
    got = lax.all_to_all(jnp.concatenate([wg, packed], axis=1), ("j", "doc"), 0, 0)
    got = got.reshape(SEGS, docs, 33, 128)
    wsum = jnp.sum(got[:, :, :32].astype(F32), axis=1).reshape(shards, 16, 128)
    csum = jnp.sum(joined(got[:, :, 32, :quarter], got[:, :, 32, quarter:]), axis=1)
    csum = jnp.broadcast_to(csum.reshape(1, 4, 128), (shards, 4, 128))
    got = lax.all_to_all(jnp.concatenate((wsum.astype(BF16),) + split(csum), axis=1), "z", 0, 0)
    (ig,) = call(
        functools.partial(taps_kernel, steps),
        "taps",
        (shape((SEGS, steps, block), BF16),),
        (at, gc, head, conv_taps),
        [pltpu.VMEM((ROWS + 3 * SEGS, block), F32)],
    )
    wsum = jnp.sum(got[:, :16].astype(F32), axis=0)
    csum = jnp.sum(joined(got[:, 16:20], got[:, 20:]), axis=0)
    send, ig = lax.optimization_barrier((jnp.concatenate([wsum, csum], axis=0), ig))
    tiles = lax.all_to_all(jnp.broadcast_to(send[None], (docs, 20, 128)), "doc", 0, 0)
    csum = tiles[:, 16:].reshape(docs, SEGS, quarter).transpose(1, 0, 2).reshape(SEGS, block)
    csum = jnp.broadcast_to(jnp.concatenate(split(csum), axis=0)[None], (SEGS, 2 * SEGS, block))
    got = lax.all_to_all(jnp.concatenate([ig, csum], axis=1), "j", 0, 0)
    return pl.pallas_call(
        functools.partial(unpack_kernel, steps),
        out_shape=(
            shape((1, steps, width), BF16), shape((share, block), F32), shape((share, block), F32), shape((SEGS, width), F32)
        ),
        in_specs=[vmem] * 2,
        out_specs=(vmem,) * 4,
        compiler_params=limit,
        name="unpack",
    )(got, tiles)


def solution(mesh):
    seq, docs = mesh.shape["seq"], mesh.shape["doc"]
    shards = seq // SEGS
    fine = Mesh(mesh.devices.reshape(shards, SEGS, docs), ("z", "j", "doc"))
    tokens, rows = P("doc", ("z", "j"), None), P(("z", "j"), None)
    return jax.shard_map(
        functools.partial(per_device, shards, docs),
        mesh=fine,
        in_specs=(tokens, tokens, rows, rows, P(), P(), P(), P()),
        out_specs=(tokens, rows, rows, P()),
        check_vma=False,
    )
```

```python
import functools

import jax
import jax.numpy as jnp
from jax import lax
from jax.experimental import pallas as pl
from jax.experimental.pallas import tpu as pltpu
from jax.sharding import Mesh
from jax.sharding import PartitionSpec as P

QFLOOR = 0.001
SEGS = 8
SPAN = 32
ROWS = SEGS * SPAN
UNROLL = (True, True, True, True)
F32 = jnp.float32
BF16 = jnp.bfloat16


def dot(a, b, contract=((1,), (0,))):
    return lax.dot_general(a, b, (contract, ((), ())), preferred_element_type=F32)


def shuffle_matrix():
    row = lax.broadcasted_iota(jnp.int32, (ROWS, ROWS), 0)
    col = lax.broadcasted_iota(jnp.int32, (ROWS, ROWS), 1)
    return jnp.where(col == (row % SEGS) * SPAN + row // SEGS, 1.0, 0.0).astype(BF16)


def by_step(buf_ref, shuffle, first):
    tiles = [buf_ref[s, pl.ds(first, SPAN), :] for s in range(SEGS)]
    return dot(shuffle, jnp.concatenate(tiles, axis=0))


def load_weights(buf_ref, w_ref, first):
    block = w_ref.shape[0]
    for s in range(SEGS):
        for p in range(2):
            for w in range(2):
                row, at = p * (block // 2) + s * 16, first + (p * 2 + w) * 16
                w_ref[row : row + 16, w * block : (w + 1) * block] = buf_ref[s, at : at + 16, :]


def one_minus_square(a, decay):
    x = 2.0 * decay
    series = x * (1.0 - x * (1 / 2) * (1.0 - x * (1 / 3)))
    return jnp.where(x < 0.0078125, series, 1.0 - a * a)


def sigmoid(x):
    return pl.reciprocal(1.0 + jnp.exp(-x), approx=True)


def block_params(at_ref, bias_ref, taps_ref, cbias_ref, decay_ref, block):
    lanes = pl.ds(pl.multiple_of(at_ref[1] * block, block), block)
    rate = jax.nn.softplus(-decay_ref[:, lanes])
    return bias_ref[:, lanes], taps_ref[:, lanes], cbias_ref[:, lanes], rate


def forward_kernel(
    steps, at_ref, buf_ref, halo_ref, bias_ref, taps_ref, cbias_ref, decay_ref,
    conv_ref, r_ref, i_ref, a_ref, m_ref, xpad_ref, seg_ref, sum_ref, w_ref,
):
    block = w_ref.shape[0]
    shuffle = shuffle_matrix()
    load_weights(buf_ref, w_ref, 2 * steps)
    bias, taps, cbias, rate = block_params(at_ref, bias_ref, taps_ref, cbias_ref, decay_ref, block)
    rate8 = 8.0 * rate
    last = by_step(buf_ref, shuffle, steps - SPAN)[ROWS - 3 * SEGS :]
    halo = jnp.where(at_ref[0] > 0, halo_ref[...], 0.0)
    for k in range(3):
        rows = last[k * SEGS : (k + 1) * SEGS]
        xpad_ref[k * SEGS : (k + 1) * SEGS, :] = jnp.concatenate(
            [halo[k : k + 1], rows[: SEGS - 1]], axis=0
        )

    def chunk(c, carry):
        prod, state, start = carry
        base = pl.multiple_of(c * ROWS, ROWS)
        first = pl.multiple_of(c * SPAN, SPAN)
        x = by_step(buf_ref, shuffle, first)
        d = by_step(buf_ref, shuffle, steps + first)
        xpad_ref[pl.ds(base + 3 * SEGS, ROWS), :] = x
        conv = cbias + taps[0:1] * x
        for k in range(1, 4):
            conv = conv + taps[k : k + 1] * xpad_ref[pl.ds(base + (3 - k) * SEGS, ROWS), :]
        conv_b = conv.astype(BF16)
        conv_ref[pl.ds(base, ROWS), :] = conv_b
        conv_v = conv_b.astype(F32)
        pre = dot(conv_b, w_ref[...])
        r = sigmoid(pre[:, :block] + bias[0:1])
        i = sigmoid(pre[:, block:] + bias[1:2])
        decay = r * rate8
        a = jnp.exp(-decay)
        q = one_minus_square(a, decay)
        m = q * lax.rsqrt(jnp.maximum(q, 1e-37))
        r_ref[pl.ds(base, ROWS), :] = r
        i_ref[pl.ds(base, ROWS), :] = i
        a_ref[pl.ds(base, ROWS), :] = a
        m_ref[pl.ds(base, ROWS), :] = m
        normed = conv_v * i * m
        for s in range(SPAN):
            rows = slice(s * SEGS, (s + 1) * SEGS)
            prod = prod * a[rows]
            state = a[rows] * state + normed[rows]
            start = start + prod * d[rows]
        return prod, state, start

    zero = jnp.zeros((SEGS, block), F32)
    prod, state, start = lax.fori_loop(0, steps // SPAN, chunk, (zero + 1.0, zero, zero), unroll=UNROLL[0])
    seg_ref[0:SEGS, :] = prod
    seg_ref[SEGS : 2 * SEGS, :] = state
    seg_ref[2 * SEGS : 3 * SEGS, :] = start
    whole, end, begin = prod[0:1], state[0:1], start[SEGS - 1 : SEGS]
    for s in range(1, SEGS):
        whole = whole * prod[s : s + 1]
        end = prod[s : s + 1] * end + state[s : s + 1]
        back = SEGS - 1 - s
        begin = start[back : back + 1] + prod[back : back + 1] * begin
    summary = jnp.concatenate([whole, end, begin], axis=1)
    for k in range(sum_ref.shape[0]):
        sum_ref[k] = summary


def backward_kernel(
    steps, shards, at_ref, buf_ref, all_ref, seg_ref, conv_ref, r_ref, i_ref, a_ref, m_ref, xpad_ref, w_ref, decay_ref,
    gc_ref, wg_ref, rows_ref,
    prev_ref, gates_ref,
):
    block = w_ref.shape[0]
    shuffle = shuffle_matrix()
    mine = at_ref[0]
    decay = decay_ref[:, pl.ds(pl.multiple_of(at_ref[1] * block, block), block)]
    rate = jax.nn.softplus(-decay)
    entering = jnp.zeros((1, block), F32)
    carry_in = jnp.zeros((1, block), F32)
    for k in range(shards):
        part = all_ref[k]
        entering = jnp.where(k < mine, part[:, :block] * entering + part[:, block : 2 * block], entering)
        back = shards - 1 - k
        part = all_ref[back]
        carry_in = jnp.where(back > mine, part[:, :block] * carry_in + part[:, 2 * block :], carry_in)
    heads, tails = [entering], [carry_in]
    for s in range(SEGS - 1):
        heads.append(seg_ref[s : s + 1] * heads[-1] + seg_ref[SEGS + s : SEGS + s + 1])
        back = SEGS - 1 - s
        tails.append(seg_ref[2 * SEGS + back : 2 * SEGS + back + 1] + seg_ref[back : back + 1] * tails[-1])
    state = jnp.concatenate(heads, axis=0)
    carry = jnp.concatenate(tails[::-1], axis=0)

    def ahead(c, state):
        rows = pl.ds(pl.multiple_of(c * ROWS, ROWS), ROWS)
        a, m = a_ref[rows, :], m_ref[rows, :]
        ci = conv_ref[rows, :].astype(F32) * i_ref[rows, :]
        normed = ci * m
        before = []
        for s in range(SPAN):
            at = slice(s * SEGS, (s + 1) * SEGS)
            before.append(state)
            state = a[at] * state + normed[at]
        direct = ci * a * lax.rsqrt(jnp.maximum(m * m, QFLOOR))
        prev_ref[rows, :] = a * (jnp.concatenate(before, axis=0) - direct)
        return state

    lax.fori_loop(0, steps // SPAN, ahead, state, unroll=UNROLL[1])

    def folded(v):
        return jnp.sum(v.reshape(SPAN, SEGS, block), axis=0)

    def back(k, held):
        carry, totals = held
        c = steps // SPAN - 1 - k
        base = pl.multiple_of(c * ROWS, ROWS)
        rows = pl.ds(base, ROWS)
        d = by_step(buf_ref, shuffle, steps + pl.multiple_of(c * SPAN, SPAN))
        a = a_ref[rows, :]
        grads = [None] * SPAN
        for s in range(SPAN - 1, -1, -1):
            at = slice(s * SEGS, (s + 1) * SEGS)
            grads[s] = d[at] + carry
            carry = a[at] * grads[s]
        g = jnp.concatenate(grads, axis=0)
        r, i = r_ref[rows, :], i_ref[rows, :]
        glr = g * prev_ref[rows, :] * (8.0 * r)
        gpr = (glr * ((r - 1.0) * rate)).astype(BF16)
        gim = g * (i * m_ref[rows, :])
        gpi = (gim * (conv_ref[rows, :].astype(F32) * (1.0 - i))).astype(BF16)
        both = jnp.concatenate([gpr, gpi], axis=1)
        gates_ref[rows, :] = both
        gc = gim + dot(both, w_ref[...], ((1,), (1,)))
        gc_ref[rows, :] = gc
        new = [folded(gc * xpad_ref[pl.ds(base + (3 - k) * SEGS, ROWS), :]) for k in range(4)]
        new += [folded(gc), folded(gpr.astype(F32)), folded(gpi.astype(F32)), folded(glr)]
        return carry, tuple(t + n for t, n in zip(totals, new, strict=True))

    zero = jnp.zeros((SEGS, block), F32)
    _, totals = lax.fori_loop(0, steps // SPAN, back, (carry, (zero,) * 8), unroll=UNROLL[2])
    sums = [jnp.sum(t, axis=0, keepdims=True) for t in totals]
    sums[7] = sums[7] * jax.nn.sigmoid(-decay)
    rows_ref[...] = jnp.concatenate(sums, axis=0)
    wg = dot(conv_ref[...], gates_ref[...], ((0,), (0,)))
    for s in range(SEGS):
        for q in range(4):
            for p in range(2):
                row = p * (block // 2) + s * 16
                tile = wg[row : row + 16, q * 128 : (q + 1) * 128]
                wg_ref[s * 4 + q, p * 16 : (p + 1) * 16, :] = tile.astype(BF16)


def taps_kernel(steps, at_ref, gc_ref, head_ref, taps_ref, ig_ref, tail_ref):
    block = gc_ref.shape[1]
    shuffle = shuffle_matrix()
    taps = taps_ref[:, pl.ds(pl.multiple_of(at_ref[1] * block, block), block)]
    final = steps // SPAN - 1
    tail_ref[:ROWS, :] = gc_ref[final * ROWS :, :]
    for k in range(3):
        rows = gc_ref[k * SEGS + 1 : (k + 1) * SEGS, :]
        tail_ref[ROWS + k * SEGS : ROWS + (k + 1) * SEGS, :] = jnp.concatenate([rows, head_ref[k : k + 1, :]], axis=0)

    def put(ref, base, first):
        xgrad = taps[0:1] * ref[pl.ds(base, ROWS), :]
        for k in range(1, 4):
            xgrad = xgrad + taps[k : k + 1] * ref[pl.ds(base + k * SEGS, ROWS), :]
        tiles = dot(shuffle, xgrad.astype(BF16), ((0,), (0,))).astype(BF16)
        for s in range(SEGS):
            ig_ref[s, pl.ds(first, SPAN), :] = tiles[s * SPAN : (s + 1) * SPAN]

    def turn(c, _):
        put(gc_ref, pl.multiple_of(c * ROWS, ROWS), pl.multiple_of(c * SPAN, SPAN))
        return 0

    lax.fori_loop(0, final, turn, 0, unroll=UNROLL[3])
    put(tail_ref, 0, final * SPAN)


def unpack_kernel(steps, got_ref, tiles_ref, ig_ref, recur_ref, input_ref, rows_ref):
    block = got_ref.shape[2]
    for half in range(2):
        recur_ref[:, half * 128 : (half + 1) * 128] = tiles_ref[half, :16, :]
        input_ref[:, half * 128 : (half + 1) * 128] = tiles_ref[2 + half, :16, :]
    for b in range(SEGS):
        ig_ref[0, :, b * block : (b + 1) * block] = got_ref[b, :steps, :]
        pair = got_ref[b, steps : steps + 2 * SEGS, :].astype(F32)
        row = pair[:SEGS] + pair[SEGS:]
        for k in range(SEGS):
            rows_ref[b : b + 1, k * block : (k + 1) * block] = row[k : k + 1]


def split(v):
    high = lax.reduce_precision(v, 8, 7)
    return high.astype(BF16), (v - high).astype(BF16)


def joined(high, low):
    return high.astype(F32) + low.astype(F32)


def per_device(
    shards, docs, block_input, state_cotangent, recur_weight, input_weight, gate_bias, conv_taps, conv_bias, decay_param
):
    steps, width = block_input.shape[1:]
    block = recur_weight.shape[1]
    share = recur_weight.shape[0]
    z, j = lax.axis_index("z"), lax.axis_index("j")
    at = jnp.stack([z, j]).astype(jnp.int32)
    params = (gate_bias, conv_taps, conv_bias[None], decay_param[None])

    weights = jnp.concatenate([recur_weight, input_weight], axis=0)
    weights = jnp.broadcast_to(weights[None], (shards, 2 * share, block))
    weights = lax.all_to_all(weights, "z", 0, 0).reshape(SEGS, 4 * share, block)
    halo = lax.ppermute(block_input[0, steps - 3 :], "z", [(k, k + 1) for k in range(shards - 1)])
    halo = jnp.pad(halo, ((0, 5), (0, 0)))
    tokens = (block_input[0], state_cotangent[0], halo)
    xs, ds, halo = (v.reshape(-1, SEGS, block).transpose(1, 0, 2) for v in tokens)
    at, weights = lax.optimization_barrier((at, weights))
    buf = lax.all_to_all(jnp.concatenate([xs, ds, weights, halo], axis=1), "j", 0, 0)
    halo = buf[SEGS - 1, 2 * steps + 4 * share :].astype(F32)

    total = SEGS * steps
    smem = pl.BlockSpec(memory_space=pltpu.SMEM)
    vmem = pl.BlockSpec(memory_space=pltpu.VMEM)
    shape = jax.ShapeDtypeStruct
    limit = pltpu.CompilerParams(vmem_limit_bytes=12 * 1024 * 1024)
    cost = pl.CostEstimate(flops=200 * total * block, bytes_accessed=12 * total * block, transcendentals=0)
    full, half = pltpu.VMEM((total, block), F32), pltpu.VMEM((total, block), BF16)

    def call(kernel, name, out_shape, operands, scratch=()):
        return pl.pallas_call(
            kernel,
            out_shape=out_shape,
            in_specs=[smem] + [vmem] * (len(operands) - 1),
            out_specs=(vmem,) * len(out_shape),
            scratch_shapes=scratch,
            compiler_params=limit,
            cost_estimate=cost,
            name=name,
        )(*operands)

    conv, r, i, a, m, xpad, seg, summary, w = call(
        functools.partial(forward_kernel, steps),
        "forward",
        (half, full, full, full, full, pltpu.VMEM((total + 3 * SEGS, block), F32), shape((3 * SEGS, block), F32))
        + (shape((shards, 1, 3 * block), F32), shape((block, 2 * block), BF16)),
        (at, buf, halo, *params),
    )
    everyone = lax.all_to_all(summary, "z", 0, 0)
    gc, wg, rows = call(
        functools.partial(backward_kernel, steps, shards),
        "backward",
        (full, shape((4 * SEGS, 32, 128), BF16), shape((8, block), F32)),
        (at, buf, everyone, seg, conv, r, i, a, m, xpad, w, params[3]),
        [pltpu.VMEM((total, block), F32), pltpu.VMEM((total, 2 * block), BF16)],
    )
    head = gc[: 3 * SEGS].reshape(3, SEGS, block)[:, 0]
    head = lax.ppermute(head, "z", [(k + 1, k) for k in range(shards - 1)])
    quarter = block // docs
    packed = jnp.concatenate(split(rows.reshape(SEGS * docs, 1, quarter)), axis=2)
    got = lax.all_to_all(jnp.concatenate([wg, packed], axis=1), ("j", "doc"), 0, 0)
    got = got.reshape(SEGS, docs, 33, 128)
    wsum = jnp.sum(got[:, :, :32].astype(F32), axis=1).reshape(shards, 16, 128)
    csum = jnp.sum(joined(got[:, :, 32, :quarter], got[:, :, 32, quarter:]), axis=1)
    csum = jnp.broadcast_to(csum.reshape(1, 4, 128), (shards, 4, 128))
    (ig,) = call(
        functools.partial(taps_kernel, steps),
        "taps",
        (shape((SEGS, steps, block), BF16),),
        (at, gc, head, conv_taps),
        [pltpu.VMEM((ROWS + 3 * SEGS, block), F32)],
    )
    send, ig = lax.optimization_barrier((jnp.concatenate((wsum.astype(BF16),) + split(csum), axis=1), ig))
    got = lax.all_to_all(send, "z", 0, 0)
    wsum = jnp.sum(got[:, :16].astype(F32), axis=0)
    csum = jnp.sum(joined(got[:, 16:20], got[:, 20:]), axis=0)
    send = jnp.concatenate([wsum, csum], axis=0)
    tiles = lax.all_to_all(jnp.broadcast_to(send[None], (docs, 20, 128)), "doc", 0, 0)
    csum = tiles[:, 16:].reshape(docs, SEGS, quarter).transpose(1, 0, 2).reshape(SEGS, block)
    csum = jnp.broadcast_to(jnp.concatenate(split(csum), axis=0)[None], (SEGS, 2 * SEGS, block))
    got = lax.all_to_all(jnp.concatenate([ig, csum], axis=1), "j", 0, 0)
    return pl.pallas_call(
        functools.partial(unpack_kernel, steps),
        out_shape=(
            shape((1, steps, width), BF16), shape((share, block), F32), shape((share, block), F32), shape((SEGS, width), F32)
        ),
        in_specs=[vmem] * 2,
        out_specs=(vmem,) * 4,
        compiler_params=limit,
        name="unpack",
    )(got, tiles)


def solution(mesh):
    seq, docs = mesh.shape["seq"], mesh.shape["doc"]
    shards = seq // SEGS
    fine = Mesh(mesh.devices.reshape(shards, SEGS, docs), ("z", "j", "doc"))
    tokens, rows = P("doc", ("z", "j"), None), P(("z", "j"), None)
    return jax.shard_map(
        functools.partial(per_device, shards, docs),
        mesh=fine,
        in_specs=(tokens, tokens, rows, rows, P(), P(), P(), P()),
        out_specs=(tokens, rows, rows, P()),
        check_vma=False,
    )
```

```python
import functools

import jax
import jax.numpy as jnp
from jax import lax
from jax.experimental import pallas as pl
from jax.experimental.pallas import tpu as pltpu
from jax.sharding import Mesh
from jax.sharding import PartitionSpec as P

QFLOOR = 0.001
SEGS = 8
SPAN = 32
ROWS = SEGS * SPAN
UNROLL = (True, True, True, True)
F32 = jnp.float32
BF16 = jnp.bfloat16


def dot(a, b, contract=((1,), (0,))):
    return lax.dot_general(a, b, (contract, ((), ())), preferred_element_type=F32)


def shuffle_matrix():
    row = lax.broadcasted_iota(jnp.int32, (ROWS, ROWS), 0)
    col = lax.broadcasted_iota(jnp.int32, (ROWS, ROWS), 1)
    return jnp.where(col == (row % SEGS) * SPAN + row // SEGS, 1.0, 0.0).astype(BF16)


def by_step(buf_ref, shuffle, first):
    tiles = [buf_ref[s, pl.ds(first, SPAN), :] for s in range(SEGS)]
    return dot(shuffle, jnp.concatenate(tiles, axis=0))


def load_weights(buf_ref, w_ref, first):
    block = w_ref.shape[0]
    for s in range(SEGS):
        for p in range(2):
            for w in range(2):
                row, at = p * (block // 2) + s * 16, first + (p * 2 + w) * 16
                w_ref[row : row + 16, w * block : (w + 1) * block] = buf_ref[s, at : at + 16, :]


def one_minus_square(a, decay):
    x = 2.0 * decay
    series = x * (1.0 - x * (1 / 2) * (1.0 - x * (1 / 3)))
    return jnp.where(x < 0.0078125, series, 1.0 - a * a)


def sigmoid(x):
    return pl.reciprocal(1.0 + jnp.exp(-x), approx=True)


def block_params(at_ref, bias_ref, taps_ref, cbias_ref, decay_ref, block):
    lanes = pl.ds(pl.multiple_of(at_ref[1] * block, block), block)
    rate = jax.nn.softplus(-decay_ref[:, lanes])
    return bias_ref[:, lanes], taps_ref[:, lanes], cbias_ref[:, lanes], rate


def forward_kernel(
    steps, at_ref, buf_ref, halo_ref, bias_ref, taps_ref, cbias_ref, decay_ref,
    conv_ref, r_ref, i_ref, a_ref, m_ref, xpad_ref, seg_ref, sum_ref, w_ref,
):
    block = w_ref.shape[0]
    shuffle = shuffle_matrix()
    load_weights(buf_ref, w_ref, 2 * steps)
    bias, taps, cbias, rate = block_params(at_ref, bias_ref, taps_ref, cbias_ref, decay_ref, block)
    rate8 = 8.0 * rate
    last = by_step(buf_ref, shuffle, steps - SPAN)[ROWS - 3 * SEGS :]
    halo = jnp.where(at_ref[0] > 0, halo_ref[...], 0.0)
    for k in range(3):
        rows = last[k * SEGS : (k + 1) * SEGS]
        xpad_ref[k * SEGS : (k + 1) * SEGS, :] = jnp.concatenate(
            [halo[k : k + 1], rows[: SEGS - 1]], axis=0
        )

    def chunk(c, carry):
        prod, state, start = carry
        base = pl.multiple_of(c * ROWS, ROWS)
        first = pl.multiple_of(c * SPAN, SPAN)
        x = by_step(buf_ref, shuffle, first)
        d = by_step(buf_ref, shuffle, steps + first)
        xpad_ref[pl.ds(base + 3 * SEGS, ROWS), :] = x
        conv = cbias + taps[0:1] * x
        for k in range(1, 4):
            conv = conv + taps[k : k + 1] * xpad_ref[pl.ds(base + (3 - k) * SEGS, ROWS), :]
        conv_b = conv.astype(BF16)
        conv_ref[pl.ds(base, ROWS), :] = conv_b
        conv_v = conv_b.astype(F32)
        pre = dot(conv_b, w_ref[...])
        r = sigmoid(pre[:, :block] + bias[0:1])
        i = sigmoid(pre[:, block:] + bias[1:2])
        decay = r * rate8
        a = jnp.exp(-decay)
        q = one_minus_square(a, decay)
        m = q * lax.rsqrt(jnp.maximum(q, 1e-37))
        r_ref[pl.ds(base, ROWS), :] = r
        i_ref[pl.ds(base, ROWS), :] = i
        a_ref[pl.ds(base, ROWS), :] = a
        m_ref[pl.ds(base, ROWS), :] = m
        normed = conv_v * i * m
        for s in range(SPAN):
            rows = slice(s * SEGS, (s + 1) * SEGS)
            prod = prod * a[rows]
            state = a[rows] * state + normed[rows]
            start = start + prod * d[rows]
        return prod, state, start

    zero = jnp.zeros((SEGS, block), F32)
    prod, state, start = lax.fori_loop(0, steps // SPAN, chunk, (zero + 1.0, zero, zero), unroll=UNROLL[0])
    seg_ref[0:SEGS, :] = prod
    seg_ref[SEGS : 2 * SEGS, :] = state
    seg_ref[2 * SEGS : 3 * SEGS, :] = start
    whole, end, begin = prod[0:1], state[0:1], start[SEGS - 1 : SEGS]
    for s in range(1, SEGS):
        whole = whole * prod[s : s + 1]
        end = prod[s : s + 1] * end + state[s : s + 1]
        back = SEGS - 1 - s
        begin = start[back : back + 1] + prod[back : back + 1] * begin
    summary = jnp.concatenate([whole, end, begin], axis=1)
    for k in range(sum_ref.shape[0]):
        sum_ref[k] = summary


def backward_kernel(
    steps, shards, at_ref, buf_ref, all_ref, seg_ref, conv_ref, r_ref, i_ref, a_ref, m_ref, xpad_ref, w_ref, decay_ref,
    gc_ref, wg_ref, rows_ref,
    prev_ref, gates_ref,
):
    block = w_ref.shape[0]
    shuffle = shuffle_matrix()
    mine = at_ref[0]
    decay = decay_ref[:, pl.ds(pl.multiple_of(at_ref[1] * block, block), block)]
    rate = jax.nn.softplus(-decay)
    entering = jnp.zeros((1, block), F32)
    carry_in = jnp.zeros((1, block), F32)
    for k in range(shards):
        part = all_ref[k]
        entering = jnp.where(k < mine, part[:, :block] * entering + part[:, block : 2 * block], entering)
        back = shards - 1 - k
        part = all_ref[back]
        carry_in = jnp.where(back > mine, part[:, :block] * carry_in + part[:, 2 * block :], carry_in)
    heads, tails = [entering], [carry_in]
    for s in range(SEGS - 1):
        heads.append(seg_ref[s : s + 1] * heads[-1] + seg_ref[SEGS + s : SEGS + s + 1])
        back = SEGS - 1 - s
        tails.append(seg_ref[2 * SEGS + back : 2 * SEGS + back + 1] + seg_ref[back : back + 1] * tails[-1])
    state = jnp.concatenate(heads, axis=0)
    carry = jnp.concatenate(tails[::-1], axis=0)

    def ahead(c, state):
        rows = pl.ds(pl.multiple_of(c * ROWS, ROWS), ROWS)
        a, m = a_ref[rows, :], m_ref[rows, :]
        ci = conv_ref[rows, :].astype(F32) * i_ref[rows, :]
        normed = ci * m
        before = []
        for s in range(SPAN):
            at = slice(s * SEGS, (s + 1) * SEGS)
            before.append(state)
            state = a[at] * state + normed[at]
        direct = ci * a * lax.rsqrt(jnp.maximum(m * m, QFLOOR))
        prev_ref[rows, :] = a * (jnp.concatenate(before, axis=0) - direct)
        return state

    lax.fori_loop(0, steps // SPAN, ahead, state, unroll=UNROLL[1])

    def folded(v):
        return jnp.sum(v.reshape(SPAN, SEGS, block), axis=0)

    def back(k, held):
        carry, totals = held
        c = steps // SPAN - 1 - k
        base = pl.multiple_of(c * ROWS, ROWS)
        rows = pl.ds(base, ROWS)
        d = by_step(buf_ref, shuffle, steps + pl.multiple_of(c * SPAN, SPAN))
        a = a_ref[rows, :]
        grads = [None] * SPAN
        for s in range(SPAN - 1, -1, -1):
            at = slice(s * SEGS, (s + 1) * SEGS)
            grads[s] = d[at] + carry
            carry = a[at] * grads[s]
        g = jnp.concatenate(grads, axis=0)
        r, i = r_ref[rows, :], i_ref[rows, :]
        glr = g * prev_ref[rows, :] * (8.0 * r)
        gpr = (glr * ((r - 1.0) * rate)).astype(BF16)
        gim = g * (i * m_ref[rows, :])
        gpi = (gim * (conv_ref[rows, :].astype(F32) * (1.0 - i))).astype(BF16)
        both = jnp.concatenate([gpr, gpi], axis=1)
        gates_ref[rows, :] = both
        gc = gim + dot(both, w_ref[...], ((1,), (1,)))
        gc_ref[rows, :] = gc
        new = [folded(gc * xpad_ref[pl.ds(base + (3 - k) * SEGS, ROWS), :]) for k in range(4)]
        new += [folded(gc), folded(gpr.astype(F32)), folded(gpi.astype(F32)), folded(glr)]
        return carry, tuple(t + n for t, n in zip(totals, new, strict=True))

    zero = jnp.zeros((SEGS, block), F32)
    _, totals = lax.fori_loop(0, steps // SPAN, back, (carry, (zero,) * 8), unroll=UNROLL[2])
    sums = [jnp.sum(t, axis=0, keepdims=True) for t in totals]
    sums[7] = sums[7] * jax.nn.sigmoid(-decay)
    rows_ref[...] = jnp.concatenate(sums, axis=0)
    wg = dot(conv_ref[...], gates_ref[...], ((0,), (0,)))
    for s in range(SEGS):
        for q in range(4):
            for p in range(2):
                row = p * (block // 2) + s * 16
                tile = wg[row : row + 16, q * 128 : (q + 1) * 128]
                wg_ref[s * 4 + q, p * 16 : (p + 1) * 16, :] = tile.astype(BF16)


def taps_kernel(steps, at_ref, gc_ref, head_ref, taps_ref, ig_ref, tail_ref):
    block = gc_ref.shape[1]
    shuffle = shuffle_matrix()
    taps = taps_ref[:, pl.ds(pl.multiple_of(at_ref[1] * block, block), block)]
    final = steps // SPAN - 1
    tail_ref[:ROWS, :] = gc_ref[final * ROWS :, :]
    for k in range(3):
        rows = gc_ref[k * SEGS + 1 : (k + 1) * SEGS, :]
        tail_ref[ROWS + k * SEGS : ROWS + (k + 1) * SEGS, :] = jnp.concatenate([rows, head_ref[k : k + 1, :]], axis=0)

    def put(ref, base, first):
        xgrad = taps[0:1] * ref[pl.ds(base, ROWS), :]
        for k in range(1, 4):
            xgrad = xgrad + taps[k : k + 1] * ref[pl.ds(base + k * SEGS, ROWS), :]
        tiles = dot(shuffle, xgrad.astype(BF16), ((0,), (0,))).astype(BF16)
        for s in range(SEGS):
            ig_ref[s, pl.ds(first, SPAN), :] = tiles[s * SPAN : (s + 1) * SPAN]

    def turn(c, _):
        put(gc_ref, pl.multiple_of(c * ROWS, ROWS), pl.multiple_of(c * SPAN, SPAN))
        return 0

    lax.fori_loop(0, final, turn, 0, unroll=UNROLL[3])
    put(tail_ref, 0, final * SPAN)


def unpack_kernel(steps, got_ref, tiles_ref, all_ref, ig_ref, recur_ref, input_ref, rows_ref):
    block = got_ref.shape[2]
    for half in range(2):
        recur_ref[:, half * 128 : (half + 1) * 128] = tiles_ref[half, :16, :]
        input_ref[:, half * 128 : (half + 1) * 128] = tiles_ref[2 + half, :16, :]
    for b in range(SEGS):
        ig_ref[0, :, b * block : (b + 1) * block] = got_ref[b, :steps, :]
        for k in range(SEGS):
            rows_ref[b : b + 1, k * block : (k + 1) * block] = all_ref[b, k : k + 1, :]


def split(v):
    high = lax.reduce_precision(v, 8, 7)
    return high.astype(BF16), (v - high).astype(BF16)


def joined(high, low):
    return high.astype(F32) + low.astype(F32)


def per_device(
    shards, docs, block_input, state_cotangent, recur_weight, input_weight, gate_bias, conv_taps, conv_bias, decay_param
):
    steps, width = block_input.shape[1:]
    block = recur_weight.shape[1]
    share = recur_weight.shape[0]
    z, j = lax.axis_index("z"), lax.axis_index("j")
    at = jnp.stack([z, j]).astype(jnp.int32)
    params = (gate_bias, conv_taps, conv_bias[None], decay_param[None])

    weights = jnp.concatenate([recur_weight, input_weight], axis=0)
    weights = jnp.broadcast_to(weights[None], (shards, 2 * share, block))
    weights = lax.all_to_all(weights, "z", 0, 0).reshape(SEGS, 4 * share, block)
    halo = lax.ppermute(block_input[0, steps - 3 :], "z", [(k, k + 1) for k in range(shards - 1)])
    halo = jnp.pad(halo, ((0, 5), (0, 0)))
    tokens = (block_input[0], state_cotangent[0], halo)
    xs, ds, halo = (v.reshape(-1, SEGS, block).transpose(1, 0, 2) for v in tokens)
    at, weights = lax.optimization_barrier((at, weights))
    buf = lax.all_to_all(jnp.concatenate([xs, ds, weights, halo], axis=1), "j", 0, 0)
    halo = buf[SEGS - 1, 2 * steps + 4 * share :].astype(F32)

    total = SEGS * steps
    smem = pl.BlockSpec(memory_space=pltpu.SMEM)
    vmem = pl.BlockSpec(memory_space=pltpu.VMEM)
    shape = jax.ShapeDtypeStruct
    limit = pltpu.CompilerParams(vmem_limit_bytes=12 * 1024 * 1024)
    cost = pl.CostEstimate(flops=200 * total * block, bytes_accessed=12 * total * block, transcendentals=0)
    full, half = pltpu.VMEM((total, block), F32), pltpu.VMEM((total, block), BF16)

    def call(kernel, name, out_shape, operands, scratch=()):
        return pl.pallas_call(
            kernel,
            out_shape=out_shape,
            in_specs=[smem] + [vmem] * (len(operands) - 1),
            out_specs=(vmem,) * len(out_shape),
            scratch_shapes=scratch,
            compiler_params=limit,
            cost_estimate=cost,
            name=name,
        )(*operands)

    conv, r, i, a, m, xpad, seg, summary, w = call(
        functools.partial(forward_kernel, steps),
        "forward",
        (half, full, full, full, full, pltpu.VMEM((total + 3 * SEGS, block), F32), shape((3 * SEGS, block), F32))
        + (shape((shards, 1, 3 * block), F32), shape((block, 2 * block), BF16)),
        (at, buf, halo, *params),
    )
    everyone = lax.all_to_all(summary, "z", 0, 0)
    gc, wg, rows = call(
        functools.partial(backward_kernel, steps, shards),
        "backward",
        (full, shape((4 * SEGS, 32, 128), BF16), shape((8, block), F32)),
        (at, buf, everyone, seg, conv, r, i, a, m, xpad, w, params[3]),
        [pltpu.VMEM((total, block), F32), pltpu.VMEM((total, 2 * block), BF16)],
    )
    head = gc[: 3 * SEGS].reshape(3, SEGS, block)[:, 0]
    head = lax.ppermute(head, "z", [(k + 1, k) for k in range(shards - 1)])
    quarter = block // docs
    packed = jnp.concatenate(split(rows.reshape(SEGS * docs, 1, quarter)), axis=2)
    got = lax.all_to_all(jnp.concatenate([wg, packed], axis=1), ("j", "doc"), 0, 0)
    got = got.reshape(SEGS, docs, 33, 128)
    wsum = jnp.sum(got[:, :, :32].astype(F32), axis=1).reshape(shards, 16, 128)
    csum = jnp.sum(joined(got[:, :, 32, :quarter], got[:, :, 32, quarter:]), axis=1)
    csum = jnp.broadcast_to(csum.reshape(1, 4, 128), (shards, 4, 128))
    got = lax.all_to_all(jnp.concatenate((wsum.astype(BF16),) + split(csum), axis=1), "z", 0, 0)
    (ig,) = call(
        functools.partial(taps_kernel, steps),
        "taps",
        (shape((SEGS, steps, block), BF16),),
        (at, gc, head, conv_taps),
        [pltpu.VMEM((ROWS + 3 * SEGS, block), F32)],
    )
    wsum = jnp.sum(got[:, :16].astype(F32), axis=0)
    csum = jnp.sum(joined(got[:, 16:20], got[:, 20:]), axis=0)
    send, ig = lax.optimization_barrier((jnp.concatenate([wsum, csum], axis=0), ig))
    tiles = lax.all_to_all(jnp.broadcast_to(send[None], (docs, 20, 128)), "doc", 0, 0)
    csum = tiles[:, 16:].reshape(docs, SEGS, quarter).transpose(1, 0, 2).reshape(SEGS, block)
    csum = jnp.broadcast_to(csum.astype(BF16)[None], (SEGS, SEGS, block))
    got = lax.all_to_all(jnp.concatenate([ig, csum], axis=1), "j", 0, 0)
    rows = got[:, steps:].astype(F32)
    return pl.pallas_call(
        functools.partial(unpack_kernel, steps),
        out_shape=(
            shape((1, steps, width), BF16), shape((share, block), F32), shape((share, block), F32), shape((SEGS, width), F32)
        ),
        in_specs=[vmem] * 3,
        out_specs=(vmem,) * 4,
        compiler_params=limit,
        name="unpack",
    )(got, tiles, rows)


def solution(mesh):
    seq, docs = mesh.shape["seq"], mesh.shape["doc"]
    shards = seq // SEGS
    fine = Mesh(mesh.devices.reshape(shards, SEGS, docs), ("z", "j", "doc"))
    tokens, rows = P("doc", ("z", "j"), None), P(("z", "j"), None)
    return jax.shard_map(
        functools.partial(per_device, shards, docs),
        mesh=fine,
        in_specs=(tokens, tokens, rows, rows, P(), P(), P(), P()),
        out_specs=(tokens, rows, rows, P()),
        check_vma=False,
    )
```

```python
import functools

import jax
import jax.numpy as jnp
from jax import lax
from jax.experimental import pallas as pl
from jax.experimental.pallas import tpu as pltpu
from jax.sharding import Mesh
from jax.sharding import PartitionSpec as P

QFLOOR = 0.001
SEGS = 8
SPAN = 32
ROWS = SEGS * SPAN
UNROLL = (True, True, True, True)
F32 = jnp.float32
BF16 = jnp.bfloat16


def dot(a, b, contract=((1,), (0,))):
    return lax.dot_general(a, b, (contract, ((), ())), preferred_element_type=F32)


def shuffle_matrix():
    row = lax.broadcasted_iota(jnp.int32, (ROWS, ROWS), 0)
    col = lax.broadcasted_iota(jnp.int32, (ROWS, ROWS), 1)
    return jnp.where(col == (row % SEGS) * SPAN + row // SEGS, 1.0, 0.0).astype(BF16)


def by_step(buf_ref, shuffle, first):
    tiles = [buf_ref[s, pl.ds(first, SPAN), :] for s in range(SEGS)]
    return dot(shuffle, jnp.concatenate(tiles, axis=0))


def load_weights(buf_ref, w_ref, first):
    block = w_ref.shape[0]
    for s in range(SEGS):
        for p in range(2):
            for w in range(2):
                row, at = p * (block // 2) + s * 16, first + (p * 2 + w) * 16
                w_ref[row : row + 16, w * block : (w + 1) * block] = buf_ref[s, at : at + 16, :]


def one_minus_square(a, decay):
    x = 2.0 * decay
    series = x * (1.0 - x * (1 / 2) * (1.0 - x * (1 / 3)))
    return jnp.where(x < 0.0078125, series, 1.0 - a * a)


def sigmoid(x):
    return pl.reciprocal(1.0 + jnp.exp(-x), approx=True)


def block_params(at_ref, bias_ref, taps_ref, cbias_ref, decay_ref, block):
    lanes = pl.ds(pl.multiple_of(at_ref[1] * block, block), block)
    rate = jax.nn.softplus(-decay_ref[:, lanes])
    return bias_ref[:, lanes], taps_ref[:, lanes], cbias_ref[:, lanes], rate


def forward_kernel(
    steps, at_ref, buf_ref, halo_ref, bias_ref, taps_ref, cbias_ref, decay_ref,
    conv_ref, r_ref, i_ref, a_ref, m_ref, xpad_ref, seg_ref, sum_ref, w_ref,
):
    block = w_ref.shape[0]
    shuffle = shuffle_matrix()
    load_weights(buf_ref, w_ref, 2 * steps)
    bias, taps, cbias, rate = block_params(at_ref, bias_ref, taps_ref, cbias_ref, decay_ref, block)
    rate8 = 8.0 * rate
    last = by_step(buf_ref, shuffle, steps - SPAN)[ROWS - 3 * SEGS :]
    halo = jnp.where(at_ref[0] > 0, halo_ref[...], 0.0)
    for k in range(3):
        rows = last[k * SEGS : (k + 1) * SEGS]
        xpad_ref[k * SEGS : (k + 1) * SEGS, :] = jnp.concatenate(
            [halo[k : k + 1], rows[: SEGS - 1]], axis=0
        )

    def chunk(c, carry):
        prod, state, start = carry
        base = pl.multiple_of(c * ROWS, ROWS)
        first = pl.multiple_of(c * SPAN, SPAN)
        x = by_step(buf_ref, shuffle, first)
        d = by_step(buf_ref, shuffle, steps + first)
        xpad_ref[pl.ds(base + 3 * SEGS, ROWS), :] = x
        conv = cbias + taps[0:1] * x
        for k in range(1, 4):
            conv = conv + taps[k : k + 1] * xpad_ref[pl.ds(base + (3 - k) * SEGS, ROWS), :]
        conv_b = conv.astype(BF16)
        conv_ref[pl.ds(base, ROWS), :] = conv_b
        conv_v = conv_b.astype(F32)
        pre = dot(conv_b, w_ref[...])
        r = sigmoid(pre[:, :block] + bias[0:1])
        i = sigmoid(pre[:, block:] + bias[1:2])
        decay = r * rate8
        a = jnp.exp(-decay)
        q = one_minus_square(a, decay)
        m = q * lax.rsqrt(jnp.maximum(q, 1e-37))
        r_ref[pl.ds(base, ROWS), :] = r
        i_ref[pl.ds(base, ROWS), :] = i
        a_ref[pl.ds(base, ROWS), :] = a
        m_ref[pl.ds(base, ROWS), :] = m
        normed = conv_v * i * m
        for s in range(SPAN):
            rows = slice(s * SEGS, (s + 1) * SEGS)
            prod = prod * a[rows]
            state = a[rows] * state + normed[rows]
            start = start + prod * d[rows]
        return prod, state, start

    zero = jnp.zeros((SEGS, block), F32)
    prod, state, start = lax.fori_loop(0, steps // SPAN, chunk, (zero + 1.0, zero, zero), unroll=UNROLL[0])
    seg_ref[0:SEGS, :] = prod
    seg_ref[SEGS : 2 * SEGS, :] = state
    seg_ref[2 * SEGS : 3 * SEGS, :] = start
    whole, end, begin = prod[0:1], state[0:1], start[SEGS - 1 : SEGS]
    for s in range(1, SEGS):
        whole = whole * prod[s : s + 1]
        end = prod[s : s + 1] * end + state[s : s + 1]
        back = SEGS - 1 - s
        begin = start[back : back + 1] + prod[back : back + 1] * begin
    summary = jnp.concatenate([whole, end, begin], axis=1)
    for k in range(sum_ref.shape[0]):
        sum_ref[k] = summary


def backward_kernel(
    steps, shards, at_ref, buf_ref, all_ref, seg_ref, conv_ref, r_ref, i_ref, a_ref, m_ref, xpad_ref, w_ref, decay_ref,
    gc_ref, wg_ref, rows_ref,
    prev_ref, gates_ref,
):
    block = w_ref.shape[0]
    shuffle = shuffle_matrix()
    mine = at_ref[0]
    decay = decay_ref[:, pl.ds(pl.multiple_of(at_ref[1] * block, block), block)]
    rate = jax.nn.softplus(-decay)
    entering = jnp.zeros((1, block), F32)
    carry_in = jnp.zeros((1, block), F32)
    for k in range(shards):
        part = all_ref[k]
        entering = jnp.where(k < mine, part[:, :block] * entering + part[:, block : 2 * block], entering)
        back = shards - 1 - k
        part = all_ref[back]
        carry_in = jnp.where(back > mine, part[:, :block] * carry_in + part[:, 2 * block :], carry_in)
    heads, tails = [entering], [carry_in]
    for s in range(SEGS - 1):
        heads.append(seg_ref[s : s + 1] * heads[-1] + seg_ref[SEGS + s : SEGS + s + 1])
        back = SEGS - 1 - s
        tails.append(seg_ref[2 * SEGS + back : 2 * SEGS + back + 1] + seg_ref[back : back + 1] * tails[-1])
    state = jnp.concatenate(heads, axis=0)
    carry = jnp.concatenate(tails[::-1], axis=0)

    def ahead(c, state):
        rows = pl.ds(pl.multiple_of(c * ROWS, ROWS), ROWS)
        a, m = a_ref[rows, :], m_ref[rows, :]
        ci = conv_ref[rows, :].astype(F32) * i_ref[rows, :]
        normed = ci * m
        before = []
        for s in range(SPAN):
            at = slice(s * SEGS, (s + 1) * SEGS)
            before.append(state)
            state = a[at] * state + normed[at]
        direct = ci * a * lax.rsqrt(jnp.maximum(m * m, QFLOOR))
        prev_ref[rows, :] = a * (jnp.concatenate(before, axis=0) - direct)
        return state

    lax.fori_loop(0, steps // SPAN, ahead, state, unroll=UNROLL[1])

    def folded(v):
        return jnp.sum(v.reshape(SPAN, SEGS, block), axis=0)

    def back(k, held):
        carry, totals = held
        c = steps // SPAN - 1 - k
        base = pl.multiple_of(c * ROWS, ROWS)
        rows = pl.ds(base, ROWS)
        d = by_step(buf_ref, shuffle, steps + pl.multiple_of(c * SPAN, SPAN))
        a = a_ref[rows, :]
        grads = [None] * SPAN
        for s in range(SPAN - 1, -1, -1):
            at = slice(s * SEGS, (s + 1) * SEGS)
            grads[s] = d[at] + carry
            carry = a[at] * grads[s]
        g = jnp.concatenate(grads, axis=0)
        r, i = r_ref[rows, :], i_ref[rows, :]
        glr = g * prev_ref[rows, :] * (8.0 * r)
        gpr = (glr * ((r - 1.0) * rate)).astype(BF16)
        gim = g * (i * m_ref[rows, :])
        gpi = (gim * (conv_ref[rows, :].astype(F32) * (1.0 - i))).astype(BF16)
        both = jnp.concatenate([gpr, gpi], axis=1)
        gates_ref[rows, :] = both
        gc = gim + dot(both, w_ref[...], ((1,), (1,)))
        gc_ref[rows, :] = gc
        new = [folded(gc * xpad_ref[pl.ds(base + (3 - k) * SEGS, ROWS), :]) for k in range(4)]
        new += [folded(gc), folded(gpr.astype(F32)), folded(gpi.astype(F32)), folded(glr)]
        return carry, tuple(t + n for t, n in zip(totals, new, strict=True))

    zero = jnp.zeros((SEGS, block), F32)
    _, totals = lax.fori_loop(0, steps // SPAN, back, (carry, (zero,) * 8), unroll=UNROLL[2])
    sums = [jnp.sum(t, axis=0, keepdims=True) for t in totals]
    sums[7] = sums[7] * jax.nn.sigmoid(-decay)
    rows_ref[...] = jnp.concatenate(sums, axis=0)
    wg = dot(conv_ref[...], gates_ref[...], ((0,), (0,)))
    for s in range(SEGS):
        for q in range(4):
            for p in range(2):
                row = p * (block // 2) + s * 16
                tile = wg[row : row + 16, q * 128 : (q + 1) * 128]
                wg_ref[s * 4 + q, p * 16 : (p + 1) * 16, :] = tile.astype(BF16)


def taps_kernel(steps, at_ref, gc_ref, head_ref, taps_ref, ig_ref, tail_ref):
    block = gc_ref.shape[1]
    shuffle = shuffle_matrix()
    taps = taps_ref[:, pl.ds(pl.multiple_of(at_ref[1] * block, block), block)]
    final = steps // SPAN - 1
    tail_ref[:ROWS, :] = gc_ref[final * ROWS :, :]
    for k in range(3):
        rows = gc_ref[k * SEGS + 1 : (k + 1) * SEGS, :]
        tail_ref[ROWS + k * SEGS : ROWS + (k + 1) * SEGS, :] = jnp.concatenate([rows, head_ref[k : k + 1, :]], axis=0)

    def put(ref, base, first):
        xgrad = taps[0:1] * ref[pl.ds(base, ROWS), :]
        for k in range(1, 4):
            xgrad = xgrad + taps[k : k + 1] * ref[pl.ds(base + k * SEGS, ROWS), :]
        tiles = dot(shuffle, xgrad.astype(BF16), ((0,), (0,))).astype(BF16)
        for s in range(SEGS):
            ig_ref[s, pl.ds(first, SPAN), :] = tiles[s * SPAN : (s + 1) * SPAN]

    def turn(c, _):
        put(gc_ref, pl.multiple_of(c * ROWS, ROWS), pl.multiple_of(c * SPAN, SPAN))
        return 0

    lax.fori_loop(0, final, turn, 0, unroll=UNROLL[3])
    put(tail_ref, 0, final * SPAN)


def unpack_kernel(steps, got_ref, tiles_ref, all_ref, ig_ref, recur_ref, input_ref, rows_ref):
    block = got_ref.shape[2]
    for half in range(2):
        recur_ref[:, half * 128 : (half + 1) * 128] = tiles_ref[half, :16, :].astype(F32)
        input_ref[:, half * 128 : (half + 1) * 128] = tiles_ref[2 + half, :16, :].astype(F32)
    for b in range(SEGS):
        ig_ref[0, :, b * block : (b + 1) * block] = got_ref[b, :steps, :]
        for k in range(SEGS):
            rows_ref[b : b + 1, k * block : (k + 1) * block] = all_ref[b, k : k + 1, :]


def split(v):
    high = lax.reduce_precision(v, 8, 7)
    return high.astype(BF16), (v - high).astype(BF16)


def joined(high, low):
    return high.astype(F32) + low.astype(F32)


def per_device(
    shards, docs, block_input, state_cotangent, recur_weight, input_weight, gate_bias, conv_taps, conv_bias, decay_param
):
    steps, width = block_input.shape[1:]
    block = recur_weight.shape[1]
    share = recur_weight.shape[0]
    z, j = lax.axis_index("z"), lax.axis_index("j")
    at = jnp.stack([z, j]).astype(jnp.int32)
    params = (gate_bias, conv_taps, conv_bias[None], decay_param[None])

    weights = jnp.concatenate([recur_weight, input_weight], axis=0)
    weights = jnp.broadcast_to(weights[None], (shards, 2 * share, block))
    weights = lax.all_to_all(weights, "z", 0, 0).reshape(SEGS, 4 * share, block)
    halo = lax.ppermute(block_input[0, steps - 3 :], "z", [(k, k + 1) for k in range(shards - 1)])
    halo = jnp.pad(halo, ((0, 5), (0, 0)))
    tokens = (block_input[0], state_cotangent[0], halo)
    xs, ds, halo = (v.reshape(-1, SEGS, block).transpose(1, 0, 2) for v in tokens)
    at, weights = lax.optimization_barrier((at, weights))
    buf = lax.all_to_all(jnp.concatenate([xs, ds, weights, halo], axis=1), "j", 0, 0)
    halo = buf[SEGS - 1, 2 * steps + 4 * share :].astype(F32)

    total = SEGS * steps
    smem = pl.BlockSpec(memory_space=pltpu.SMEM)
    vmem = pl.BlockSpec(memory_space=pltpu.VMEM)
    shape = jax.ShapeDtypeStruct
    limit = pltpu.CompilerParams(vmem_limit_bytes=12 * 1024 * 1024)
    cost = pl.CostEstimate(flops=200 * total * block, bytes_accessed=12 * total * block, transcendentals=0)
    full, half = pltpu.VMEM((total, block), F32), pltpu.VMEM((total, block), BF16)

    def call(kernel, name, out_shape, operands, scratch=()):
        return pl.pallas_call(
            kernel,
            out_shape=out_shape,
            in_specs=[smem] + [vmem] * (len(operands) - 1),
            out_specs=(vmem,) * len(out_shape),
            scratch_shapes=scratch,
            compiler_params=limit,
            cost_estimate=cost,
            name=name,
        )(*operands)

    conv, r, i, a, m, xpad, seg, summary, w = call(
        functools.partial(forward_kernel, steps),
        "forward",
        (half, full, full, full, full, pltpu.VMEM((total + 3 * SEGS, block), F32), shape((3 * SEGS, block), F32))
        + (shape((shards, 1, 3 * block), F32), shape((block, 2 * block), BF16)),
        (at, buf, halo, *params),
    )
    everyone = lax.all_to_all(summary, "z", 0, 0)
    gc, wg, rows = call(
        functools.partial(backward_kernel, steps, shards),
        "backward",
        (full, shape((4 * SEGS, 32, 128), BF16), shape((8, block), F32)),
        (at, buf, everyone, seg, conv, r, i, a, m, xpad, w, params[3]),
        [pltpu.VMEM((total, block), F32), pltpu.VMEM((total, 2 * block), BF16)],
    )
    head = gc[: 3 * SEGS].reshape(3, SEGS, block)[:, 0]
    head = lax.ppermute(head, "z", [(k + 1, k) for k in range(shards - 1)])
    quarter = block // docs
    packed = jnp.concatenate(split(rows.reshape(SEGS * docs, 1, quarter)), axis=2)
    got = lax.all_to_all(jnp.concatenate([wg, packed], axis=1), ("j", "doc"), 0, 0)
    got = got.reshape(SEGS, docs, 33, 128)
    wsum = jnp.sum(got[:, :, :32].astype(F32), axis=1).reshape(shards, 16, 128)
    csum = jnp.sum(joined(got[:, :, 32, :quarter], got[:, :, 32, quarter:]), axis=1)
    csum = jnp.broadcast_to(csum.reshape(1, 4, 128), (shards, 4, 128))
    got = lax.all_to_all(jnp.concatenate((wsum.astype(BF16),) + split(csum), axis=1), "z", 0, 0)
    (ig,) = call(
        functools.partial(taps_kernel, steps),
        "taps",
        (shape((SEGS, steps, block), BF16),),
        (at, gc, head, conv_taps),
        [pltpu.VMEM((ROWS + 3 * SEGS, block), F32)],
    )
    wsum = jnp.sum(got[:, :16].astype(F32), axis=0)
    csum = jnp.sum(joined(got[:, 16:20], got[:, 20:]), axis=0)
    send, ig = lax.optimization_barrier((jnp.concatenate([wsum, csum], axis=0).astype(BF16), ig))
    tiles = lax.all_to_all(jnp.broadcast_to(send[None], (docs, 20, 128)), "doc", 0, 0)
    csum = tiles[:, 16:].reshape(docs, SEGS, quarter).transpose(1, 0, 2).reshape(SEGS, block)
    csum = jnp.broadcast_to(csum.astype(BF16)[None], (SEGS, SEGS, block))
    got = lax.all_to_all(jnp.concatenate([ig, csum], axis=1), "j", 0, 0)
    rows = got[:, steps:].astype(F32)
    return pl.pallas_call(
        functools.partial(unpack_kernel, steps),
        out_shape=(
            shape((1, steps, width), BF16), shape((share, block), F32), shape((share, block), F32), shape((SEGS, width), F32)
        ),
        in_specs=[vmem] * 3,
        out_specs=(vmem,) * 4,
        compiler_params=limit,
        name="unpack",
    )(got, tiles, rows)


def solution(mesh):
    seq, docs = mesh.shape["seq"], mesh.shape["doc"]
    shards = seq // SEGS
    fine = Mesh(mesh.devices.reshape(shards, SEGS, docs), ("z", "j", "doc"))
    tokens, rows = P("doc", ("z", "j"), None), P(("z", "j"), None)
    return jax.shard_map(
        functools.partial(per_device, shards, docs),
        mesh=fine,
        in_specs=(tokens, tokens, rows, rows, P(), P(), P(), P()),
        out_specs=(tokens, rows, rows, P()),
        check_vma=False,
    )
```
